128 devices in a mesh: alpha: 16 (over x, z), beta: 8 (over y, core).
Axes of the slice: x: 4, y: 4, z: 4, core: 2. Of those that a mesh axis runs over, the one named last changes fastest.
Arguments:
- amplitudes: bfloat16 [8192, 256], P('alpha', 'beta'), may hold values from -6 to 6
- integrals: float32 [324, 324], replicated, may hold values from -0.1 to 0.1
- beta_pair: int32 [256, 256], P('beta'), may hold values from 0 to 323
- beta_coef: float32 [256, 256], P('beta'), may hold values from -1 to 1, as said below
- pair_src: int32 [64, 4], replicated, may hold values from 0 to 63, as said below
- link_row: int32 [64, 4, 1024], P('alpha'), may hold values from 0 to 127
- link_col: int32 [64, 4, 1024], P('alpha'), may hold values from 0 to 41471
- link_coef: float32 [64, 4, 1024], P('alpha'), may hold values from -1 to 1, as said below
- link_count: int32 [64, 4], P('alpha'), may hold values from 512 to 1024, as said below
Outputs:
- sigma: float32 [8192, 256], P('alpha', 'beta')
The draws below stay inside these ranges and needn't reach their ends.
Inputs may be any that keep to these rules, and one draw needn't show every extreme that they name: `beta_coef`: each entry is -1, 0 or 1. `link_coef`: each entry is -1 or 1. `pair_src`: block b is held by alpha device b // 4. Each row names 4 different blocks. The rows of the 4 target blocks of one alpha device together name at most 2 different blocks held by any one alpha device, and exactly 2 for some holder in every draw. `link_count`: some block pair has all 1024 slots occupied in every draw.
All inputs are finite; a program needn't handle non-finite values.
Results may differ from the reference program's by a relative error of at most 0.0029.
Values may be sent and summed in bfloat16 or wider, within the bound.
A program may use at most 128 MiB of HBM per device.

```python
import jax
import jax.numpy as jnp
from jax import lax

NP = 324
ABLK = 128
BLK_DEV = 4
NB = 256
PAIRS = 4
LINKS = 1024
FETCH_CAP = 2
NBLK = 64
NA = 8192


def draw_beta_coef(key, part):
    key = jax.random.fold_in(key, 3)
    picks = jax.random.randint(key, (NB, NB), 0, 3)
    return (picks == 1).astype(jnp.float32) - (picks == 2).astype(jnp.float32)


def draw_link_coef(key, part):
    key = jax.random.fold_in(key, 5)
    picks = jax.random.randint(key, (NBLK, PAIRS, LINKS), 0, 2)
    return picks.astype(jnp.float32) * 2.0 - 1.0


def draw_link_count(key, part):
    key = jax.random.fold_in(key, 7)
    counts = jax.random.randint(key, (NBLK, PAIRS), LINKS // 2, LINKS + 1)
    return counts.at[0, 0].set(LINKS).astype(jnp.int32)


def draw_pair_src(key, part):
    key = jax.random.fold_in(key, 11)
    alpha_count = NBLK // BLK_DEV
    pool_size = alpha_count * FETCH_CAP
    first_key, second_key = jax.random.split(key)
    raw_first = jax.random.randint(first_key, (alpha_count, alpha_count, BLK_DEV), 0, 1 << 20)
    scores_first = raw_first * BLK_DEV + jnp.arange(BLK_DEV, dtype=jnp.int32)
    chosen = jnp.argsort(scores_first, axis=2, stable=True)[:, :, :FETCH_CAP]
    owner_base = (jnp.arange(alpha_count, dtype=jnp.int32) * BLK_DEV)[None, :, None]
    pool_ids = (chosen + owner_base).reshape(alpha_count, pool_size)
    raw_second = jax.random.randint(second_key, (alpha_count, BLK_DEV, pool_size), 0, 1 << 20)
    scores = raw_second * pool_size + jnp.arange(pool_size, dtype=jnp.int32)
    forced_owner = (jnp.arange(alpha_count, dtype=jnp.int32) + 1) % alpha_count
    pool_owner = jnp.arange(pool_size, dtype=jnp.int32) // FETCH_CAP
    first_target = (jnp.arange(BLK_DEV, dtype=jnp.int32) == 0)[None, :, None]
    forced = first_target & (pool_owner[None, None, :] == forced_owner[:, None, None])
    scores = scores + forced.astype(jnp.int32) * (1 << 28)
    order_idx = jnp.argsort(-scores, axis=2, stable=True)[:, :, :PAIRS]
    picked = jnp.take_along_axis(jnp.broadcast_to(pool_ids[:, None, :], (alpha_count, BLK_DEV, pool_size)), order_idx, axis=2)
    return picked.reshape(NBLK, PAIRS).astype(jnp.int32)


def place_ends(drawn, own_key, smallest, largest):
    longest = drawn.shape.index(max(drawn.shape))
    spots = []
    for shift in (0, 1):
        where = [jax.random.randint(jax.random.fold_in(own_key, axis), (), 0, length) for axis, length in enumerate(drawn.shape)]
        where[longest] = (where[longest] + shift) % drawn.shape[longest]
        spots.append(tuple(where))
    return drawn.at[spots[0]].set(smallest).at[spots[1]].set(largest)


def steps_of(rng, extent, cuts, least, top_value):
    level = 1.0
    for dim, parts in cuts:
        heights = jax.random.uniform(jax.random.fold_in(jax.random.fold_in(rng, 6), dim), (parts,), jnp.float32, least / len(cuts), top_value / len(cuts))
        level = level * jnp.repeat(jnp.exp(heights), extent[dim] // parts).reshape((-1,) + (1,) * (len(extent) - 1 - dim))
    return level


def normal_values(own_key, dims, spread, most, cuts=(), kind=jnp.bfloat16):
    drawn = spread * jax.random.normal(own_key, dims, jnp.float32)
    if cuts:
        drawn = drawn * steps_of(own_key, dims, cuts, -0.22, 0.18)
    return jnp.clip(drawn, -most, most).astype(kind)


def setup_inputs(seed: int = 0) -> dict:
    streams_of = jax.random.split(jax.random.key(seed), 10)
    amplitudes = normal_values(streams_of[0], (NA, NB), 1.0, 6.0, ((0, 16), (1, 8)))
    integrals = normal_values(streams_of[1], (NP, NP), 0.016, 0.1, (), jnp.float32)
    beta_pair = place_ends(jax.random.randint(streams_of[2], (NB, NB), 0, NP), jax.random.fold_in(streams_of[2], 1), 0, NP - 1).astype(jnp.int32)
    beta_coef = draw_beta_coef(jax.random.fold_in(streams_of[9], 71), 0)
    pair_src = draw_pair_src(jax.random.fold_in(streams_of[9], 71), 0)
    link_row = place_ends(jax.random.randint(streams_of[5], (NBLK, PAIRS, LINKS), 0, ABLK), jax.random.fold_in(streams_of[5], 1), 0, ABLK - 1).astype(jnp.int32)
    link_col = place_ends(jax.random.randint(streams_of[6], (NBLK, PAIRS, LINKS), 0, NP * ABLK), jax.random.fold_in(streams_of[6], 1), 0, (NP * ABLK) - 1).astype(jnp.int32)
    link_coef = draw_link_coef(jax.random.fold_in(streams_of[9], 71), 0)
    link_count = draw_link_count(jax.random.fold_in(streams_of[9], 71), 0)
    return {"amplitudes": amplitudes, "integrals": integrals, "beta_pair": beta_pair, "beta_coef": beta_coef, "pair_src": pair_src, "link_row": link_row, "link_col": link_col, "link_coef": link_coef, "link_count": link_count}


def reference(amplitudes, integrals, beta_pair, beta_coef, pair_src, link_row, link_col, link_coef, link_count):
    group_width = 32
    coupled = (jnp.take(integrals, beta_pair, axis=1) * beta_coef[None]).astype(jnp.bfloat16)
    coupled = lax.optimization_barrier(coupled).astype(jnp.float32)
    blocks_all = amplitudes.astype(jnp.float32).reshape(NBLK, ABLK, NB)
    filled = jnp.arange(LINKS, dtype=jnp.int32)[None, None, :] < link_count[:, :, None]
    weights = jnp.where(filled, link_coef, jnp.float32(0.0))
    targets = jnp.broadcast_to(jnp.arange(NBLK, dtype=jnp.int32)[:, None, None], link_row.shape)

    def one_group(start):
        h_part = lax.dynamic_slice_in_dim(coupled, start, group_width, 1)
        excited = jnp.einsum("kbj,naj->nkab", h_part, blocks_all, precision=lax.Precision.HIGHEST)
        flat_rows = excited.reshape(NBLK, NP * ABLK, group_width)
        picked = flat_rows[pair_src[:, :, None], link_col]
        sigma_part = jnp.zeros((NBLK, ABLK, group_width), jnp.float32)
        return sigma_part.at[targets, link_row].add(picked * weights[..., None])

    starts = (jnp.arange(NB // group_width, dtype=jnp.int32) * group_width).astype(jnp.int32)
    groups = lax.map(one_group, starts)
    return groups.transpose(1, 2, 0, 3).reshape(NBLK * ABLK, NB)
```

```python
import functools

import jax
import jax.numpy as jnp
from jax import lax
from jax.experimental import pallas as pl
from jax.experimental.pallas import tpu as pltpu
from jax.sharding import PartitionSpec as P

NP = 324
ABLK = 128
LINKS = 1024
PAIRS = 4
BLK = 4
NB = 256
HALF = 128
QUART = 81
KROWS = 88
KHI = NP - 256
KHIP = 80
CAP = 32
GROUPS = KROWS // 4
NT = (((1,), (1,)), ((), ()))
f32, bf16, i32 = jnp.float32, jnp.bfloat16, jnp.int32


def dot(a, b):
    return jnp.dot(a, b, preferred_element_type=f32)


def dot_nt(a, b):
    return lax.dot_general(a, b, NT, preferred_element_type=f32)


def iota(shape, dim):
    return lax.broadcasted_iota(i32, shape, dim)


def build_coupled(v_ref, ints_ref, coup):
    lo_ids = iota((256, 256), 0).astype(f32)
    hi_ids = iota((KHIP, 256), 0).astype(f32) + 256.0
    ints_lo = ints_ref[:, :256]
    ints_hi = ints_ref[:, 256 : 256 + KHIP]

    def one(ib, carry):
        v = v_ref[pl.ds(ib, 1), :]
        where_to = jnp.abs(v) - 1.0
        sign = jnp.where(v < 0.0, -1.0, 1.0)
        hot_lo = jnp.where(lo_ids == where_to, sign, 0.0).astype(bf16)
        hot_hi = jnp.where(hi_ids == where_to, sign, 0.0).astype(bf16)
        out = dot(ints_lo, hot_lo) + dot(ints_hi, hot_hi)
        start = pl.multiple_of(ib * KROWS, 8)
        coup[0, pl.ds(start, KROWS), :] = out[:, :128]
        coup[1, pl.ds(start, KROWS), :] = out[:, 128:]
        return carry

    lax.fori_loop(0, HALF, one, 0)


def rank_links(klq, rank):
    tri = (iota((256, 384), 0) <= iota((256, 384), 1)).astype(f32).astype(bf16)
    kl_ids = iota((KROWS, 256), 0).astype(f32)

    def one(p, carry):
        carry = list(carry)
        for c in range(4):
            hots = []
            for t in range(BLK):
                row = klq[pl.ds(t * PAIRS + p, 1), c * 256 : (c + 1) * 256]
                hots.append(kl_ids == row)
            stacked = jnp.concatenate([h.astype(f32).astype(bf16) for h in hots], axis=0)
            cum = dot(stacked, tri)
            for t in range(BLK):
                part = cum[t * KROWS : (t + 1) * KROWS]
                base = jnp.concatenate([carry[t], carry[t]], axis=1)
                mine = jnp.where(hots[t], part[:, :256] + base, 0.0)
                got = jnp.sum(mine, axis=0, keepdims=True) - 1.0
                rank[pl.ds(t * PAIRS + p, 1), c * 256 : (c + 1) * 256] = got
                carry[t] = carry[t] + part[:, 256:]
        return tuple(carry)

    zero = jnp.zeros((KROWS, 128), f32)
    lax.fori_loop(0, PAIRS, one, (zero,) * BLK)


def fill_table(lo, hi, u1, u2, t1, t2):
    lo_ids = iota((128, LINKS), 0).astype(f32)
    hi_ids = iota((32, LINKS), 0).astype(f32)

    def target(t, carry):
        a1 = jnp.zeros((128, 32), f32)
        a2 = jnp.zeros((32, 128), f32)
        for p in range(PAIRS):
            i = t * PAIRS + p
            here = lo_ids == lo[pl.ds(i, 1), :]
            v1 = jnp.where(here, u1[pl.ds(i, 1), :], 0.0).astype(bf16)
            v2 = jnp.where(here, u2[pl.ds(i, 1), :], 0.0).astype(bf16)
            group = (hi_ids == hi[pl.ds(i, 1), :]).astype(f32).astype(bf16)
            a1 = a1 + dot_nt(v1, group)
            a2 = a2 + dot_nt(group, v2)
        t1[t] = jnp.concatenate([a1, jnp.zeros((128, 96), f32)], axis=1)
        t2[t] = a2
        return carry

    lax.fori_loop(0, BLK, target, 0)


def apply_links(at_ref, coup, t1, t2, acc):
    tables = [((128 + iota((128, 128), 1)) * (1 << p)).astype(f32) for p in range(PAIRS)]
    row_ids = iota((128, 256), 0).astype(f32)

    def two(g2, carry):
        picked = []
        for h in range(2):
            g = g2 * 2 + h
            rows = []
            for t in range(BLK):
                code = jnp.take_along_axis(t1[t], jnp.full((128, 128), g, i32), axis=1)
                size = jnp.abs(code)
                sign = jnp.where(code < 0.0, -1.0, 1.0)
                hot = jnp.concatenate(
                    [jnp.where(size == tab, sign, 0.0).astype(bf16) for tab in tables], axis=1
                )
                rows.append(dot_nt(hot, at_ref[t]).astype(bf16))
            for k in range(4):
                mine = jnp.concatenate([r[k * CAP : (k + 1) * CAP] for r in rows], axis=0)
                kl = g * 4 + k
                c = jnp.concatenate(
                    [coup[j, pl.ds(kl, HALF, stride=KROWS), :].astype(bf16) for j in range(2)],
                    axis=1,
                )
                picked.append(dot_nt(mine, c).astype(bf16))
        for t in range(BLK):
            block = jnp.concatenate([q[t * CAP : (t + 1) * CAP] for q in picked], axis=0)
            to = jnp.concatenate(
                [t2[t, pl.ds(g2 * 2, 1), :], t2[t, pl.ds(g2 * 2 + 1, 1), :]], axis=1
            )
            hot = (row_ids == to).astype(f32).astype(bf16)
            acc[t] += dot(hot, block)
        return carry

    lax.fori_loop(0, GROUPS // 2, two, 0)


def kernel(at_ref, v_ref, ints_ref, kl0_ref, col_ref, row_ref, coef_ref, count_ref, out_ref,
           coup, klq, rank, lo, hi, u1, u2, t1, t2):
    build_coupled(v_ref, ints_ref, coup)
    col = col_ref[...]
    kl = (col >> 7) - kl0_ref[0]
    filled = iota((BLK * PAIRS, LINKS), 1) < count_ref[...]
    mine = filled & (kl >= 0) & (kl < QUART)
    kl = jnp.where(mine, kl, -1)
    klq[...] = kl.astype(f32)
    power = (1 << (iota((BLK * PAIRS, LINKS), 0) & 3)).astype(f32)
    u1[...] = coef_ref[...] * (128 + (col & 127)).astype(f32) * power
    u2[...] = row_ref[...].astype(f32)
    rank_links(klq, rank)
    rank[...] = jnp.where(mine, rank[...], -1.0)
    most = jnp.max(rank[...]).astype(i32)
    out_ref[...] = jnp.zeros((BLK, ABLK, HALF), f32)

    def one_round(step, carry):
        kl = klq[...].astype(i32)
        r = rank[...].astype(i32) - step * CAP
        ok = (kl >= 0) & (r >= 0) & (r < CAP)
        lo[...] = jnp.where(ok, (kl & 3) * CAP + r, -1).astype(f32)
        hi[...] = jnp.where(ok, kl >> 2, -1).astype(f32)
        fill_table(lo, hi, u1, u2, t1, t2)
        apply_links(at_ref, coup, t1, t2, out_ref)
        return carry

    lax.fori_loop(0, (most + CAP) // CAP, one_round, 0)


def body(amplitudes, integrals, beta_pair, beta_coef, pair_src, link_row, link_col, link_coef, link_count):
    me_a, me_b = lax.axis_index("alpha"), lax.axis_index("beta")
    groups = [[0, 1, 2, 3], [4, 5, 6, 7]]
    own = jnp.transpose(amplitudes.reshape(BLK, ABLK, 32), (0, 2, 1))
    every = lax.all_gather(own, "alpha", axis=0, tiled=True)
    src = lax.dynamic_slice_in_dim(pair_src, me_a * BLK, BLK, 0)
    chosen = jnp.take(every, src.reshape(-1), axis=0).reshape(BLK, PAIRS, 32, ABLK)
    chosen = jnp.transpose(chosen, (0, 2, 1, 3)).reshape(BLK, 32, PAIRS * ABLK)
    at = lax.all_gather(chosen, "beta", axis=1, tiled=True)
    code = beta_coef * (beta_pair + 1).astype(f32)
    v = lax.all_gather(code, "beta", axis=0, tiled=True, axis_index_groups=groups)
    kl0 = (me_b % 4) * QUART
    ints = lax.dynamic_slice_in_dim(integrals, kl0, QUART, 0).astype(bf16)
    ints = jnp.pad(ints, ((0, KROWS - QUART), (0, 384 - NP)))
    vm = pl.BlockSpec(memory_space=pltpu.VMEM)
    part = pl.pallas_call(
        kernel,
        out_shape=jax.ShapeDtypeStruct((BLK, ABLK, HALF), f32),
        in_specs=[vm, vm, vm, pl.BlockSpec(memory_space=pltpu.SMEM), vm, vm, vm, vm],
        out_specs=vm,
        scratch_shapes=[
            pltpu.VMEM((2, HALF * KROWS, 128), f32),
        ] + [pltpu.VMEM((BLK * PAIRS, LINKS), f32)] * 6 + [
            pltpu.VMEM((BLK, 128, 128), f32),
            pltpu.VMEM((BLK, 32, 128), f32),
        ],
        compiler_params=pltpu.CompilerParams(vmem_limit_bytes=48 << 20),
        name="links",
    )(at, v, ints, kl0.reshape(1), link_col.reshape(16, LINKS), link_row.reshape(16, LINKS),
      link_coef.reshape(16, LINKS), link_count.reshape(16, 1))
    part = part.reshape(BLK * ABLK, HALF)
    return lax.psum_scatter(part, "beta", scatter_dimension=1, tiled=True, axis_index_groups=groups)


def solution(mesh):
    in_specs = (P("alpha", "beta"), P(), P("beta", None), P("beta", None), P(),
                P("alpha", None, None), P("alpha", None, None), P("alpha", None, None), P("alpha", None))
    return jax.shard_map(body, mesh=mesh, in_specs=in_specs, out_specs=P("alpha", "beta"), check_vma=False)
```

```python
import jax
import jax.numpy as jnp
from jax import lax
from jax.experimental import pallas as pl
from jax.experimental.pallas import tpu as pltpu
from jax.sharding import PartitionSpec as P

NP = 324
ABLK = 128
LINKS = 1024
PAIRS = 4
BLK = 4
NB = 256
SLAB = 32
ALPHA = 16
HALF = 128
QUART = 81
KROWS = 88
KHIP = 80
CAP = 32
GROUPS = 21
GCHUNK = 7
NTDIMS = (((1,), (1,)), ((), ()))
f32, bf16, i32 = jnp.float32, jnp.bfloat16, jnp.int32
MESH = pl.DeviceIdType.MESH


def dot(a, b):
    return jnp.dot(a, b, preferred_element_type=f32)


def dot_nt(a, b):
    return lax.dot_general(a, b, NTDIMS, preferred_element_type=f32)


def iota(shape, dim):
    return lax.broadcasted_iota(i32, shape, dim)


def hot_bf16(mask):
    return mask.astype(f32).astype(bf16)


def my_integrals(integ, first):
    rows = hot_bf16(iota((KROWS, NP), 1) - first == iota((KROWS, NP), 0))
    rows = jnp.where(iota((KROWS, NP), 0) < QUART, rows, jnp.zeros((), bf16))
    mine = dot(rows, integ[...].astype(bf16)).astype(bf16)
    shift = hot_bf16(iota((NP, 128), 0) - 256 == iota((NP, 128), 1))
    return mine[:, :256], dot(mine, shift).astype(bf16)[:, :KHIP]


def build_coupled(v_ref, ints, coup, begin, end):
    lo_ids = iota((256, 256), 0).astype(f32)
    hi_ids = iota((KHIP, 256), 0).astype(f32) + 256.0
    ints_lo, ints_hi = ints

    def one(ib, carry):
        v = v_ref[pl.ds(ib, 1), :]
        where_to = jnp.abs(v) - 1.0
        sign = jnp.where(v < 0.0, -1.0, 1.0)
        hot_lo = jnp.where(lo_ids == where_to, sign, 0.0).astype(bf16)
        hot_hi = jnp.where(hi_ids == where_to, sign, 0.0).astype(bf16)
        out = dot(ints_lo, hot_lo) + dot(ints_hi, hot_hi)
        start = pl.multiple_of(ib * KROWS, 8)
        coup[0, pl.ds(start, KROWS), :] = out[:, :128]
        coup[1, pl.ds(start, KROWS), :] = out[:, 128:]
        return carry

    lax.fori_loop(begin, end, one, 0, unroll=16)


def rank_links(klq, rank):
    tri = hot_bf16(iota((256, 384), 0) <= iota((256, 384), 1))
    kl_ids = iota((KROWS, 256), 0).astype(f32)

    def one(p, carry):
        carry = list(carry)
        for c in range(4):
            hots = []
            for t in range(BLK):
                row = klq[pl.ds(t * PAIRS + p, 1), c * 256 : (c + 1) * 256]
                hots.append(kl_ids == row)
            stacked = jnp.concatenate([hot_bf16(h) for h in hots], axis=0)
            cum = dot(stacked, tri)
            for t in range(BLK):
                part = cum[t * KROWS : (t + 1) * KROWS]
                base = jnp.concatenate([carry[t], carry[t]], axis=1)
                mine = jnp.where(hots[t], part[:, :256] + base, 0.0)
                got = jnp.sum(mine, axis=0, keepdims=True) - 1.0
                rank[pl.ds(t * PAIRS + p, 1), c * 256 : (c + 1) * 256] = got
                carry[t] = carry[t] + part[:, 256:]
        return tuple(carry)

    zero = jnp.zeros((KROWS, 128), f32)
    lax.fori_loop(0, PAIRS, one, (zero,) * BLK)


def fill_tables(lo, hi, u1, u2, t1, t2):
    lo_ids = iota((128, LINKS), 0).astype(f32)
    hi_ids = iota((32, LINKS), 0).astype(f32)

    def target(t, carry):
        a1 = jnp.zeros((128, 32), f32)
        a2 = jnp.zeros((32, 128), f32)
        for p in range(PAIRS):
            i = t * PAIRS + p
            here = lo_ids == lo[pl.ds(i, 1), :]
            v1 = jnp.where(here, u1[pl.ds(i, 1), :], 0.0).astype(bf16)
            v2 = jnp.where(here, u2[pl.ds(i, 1), :], 0.0).astype(bf16)
            group = hot_bf16(hi_ids == hi[pl.ds(i, 1), :])
            a1 = a1 + dot_nt(v1, group)
            a2 = a2 + dot_nt(group, v2)
        t1[t] = jnp.concatenate([a1, jnp.zeros((128, 96), f32)], axis=1)
        t2[t] = a2
        return carry

    lax.fori_loop(0, BLK, target, 0)


def gather_rows(at, t1, gs):
    tables = [((128 + iota((128, 128), 1)) * (1 << p)).astype(f32) for p in range(PAIRS)]

    def one(c, carry):
        for t in range(BLK):
            hots = []
            for h in range(GCHUNK):
                code = jnp.take_along_axis(t1[t], jnp.full((128, 128), c * GCHUNK + h, i32), axis=1)
                size = jnp.abs(code)
                sign = jnp.where(code < 0.0, -1.0, 1.0)
                hots.append(
                    jnp.concatenate(
                        [jnp.where(size == tab, sign, 0.0).astype(bf16) for tab in tables], axis=1
                    )
                )
            amps = at[:, t].reshape(NB, PAIRS * ABLK)
            rows = dot_nt(jnp.concatenate(hots, axis=0), amps).astype(bf16)
            for h in range(GCHUNK):
                for k in range(4):
                    s = h * 128 + k * CAP
                    gs[(c * GCHUNK + h) * 4 + k, t * CAP : (t + 1) * CAP, :] = rows[s : s + CAP]
        return carry

    lax.fori_loop(0, GROUPS // GCHUNK, one, 0)


def pick(coup, gs, ps):
    def one(kl, carry):
        c = jnp.concatenate(
            [coup[j, pl.ds(kl, HALF, stride=KROWS), :].astype(bf16) for j in range(2)], axis=1
        )
        q = dot_nt(gs[kl], c).astype(bf16)
        start = pl.multiple_of(kl * CAP, CAP)
        for t in range(BLK):
            ps[t, pl.ds(start, CAP), :] = q[t * CAP : (t + 1) * CAP]
        return carry

    lax.fori_loop(0, QUART, one, 0, unroll=27)
    for t in range(BLK):
        ps[t, QUART * CAP :, :] = jnp.zeros((4 * CAP * GROUPS - QUART * CAP, HALF), bf16)


def add_rows(t2, ps, t):
    ids = iota((128, 128), 0).astype(f32)
    hot = jnp.concatenate([hot_bf16(ids == t2[t, g : g + 1, :]) for g in range(GROUPS)], axis=1)
    return dot(hot, ps[t])


def kernel(amp_h, integ_h, pair_h, coef_h, src, col_h, row_h, lcoef_h, count, out, at_out, flag_out,
           amp, integ, pair, coef, col, row, lcoef, own, ev, vall, at, coup, klq, rank, lo, hi, u1, u2,
           t1, t2, gs, ps, sb, rb, fl, in_sem, a_send, a_recv, v_send, v_recv, y_send, y_recv, s_send,
           s_recv, r_send, r_recv, f_send, f_recv, o_sem):
    a, b = lax.axis_index("alpha"), lax.axis_index("beta")
    y, core = b // 2, b % 2
    first, q = b // 4 * 4, b % 4
    sibling = y * 2 + 1 - core
    mates = [first + (q + k) % 4 for k in range(1, 4)]
    rings = [(y + k) % 4 * 2 + core for k in range(1, 4)]
    back = [(y + 4 - k) % 4 * 2 + core for k in range(1, 4)]

    loads = []
    for n, (h, m) in enumerate([(amp_h, amp), (pair_h, pair), (coef_h, coef), (col_h, col), (row_h, row),
                                (lcoef_h, lcoef), (integ_h, integ)]):
        loads.append(pltpu.make_async_copy(h, m, in_sem.at[n]))
        loads[-1].start()

    barrier = pltpu.get_barrier_semaphore()
    for k in range(1, ALPHA):
        pl.semaphore_signal(barrier, inc=1, device_id=((a + k) % ALPHA, b), device_id_type=MESH)
    for k in range(1, 8):
        pl.semaphore_signal(barrier, inc=1, device_id=(a, (b + k) % 8), device_id_type=MESH)

    loads[0].wait()
    eye = hot_bf16(iota((SLAB, SLAB), 0) == iota((SLAB, SLAB), 1))
    for j in range(BLK):
        own[j] = dot_nt(eye, amp[j * ABLK : (j + 1) * ABLK, :]).astype(bf16)
    loads[1].wait()
    loads[2].wait()
    mine = pl.ds(pl.multiple_of(q * SLAB, SLAB), SLAB)
    vall[mine, :] = coef[...] * (pair[...] + 1).astype(f32)
    pl.semaphore_wait(barrier, ALPHA - 1 + 7)

    def remote(source, target, send, recv, to):
        c = pltpu.make_async_remote_copy(src_ref=source, dst_ref=target, send_sem=send, recv_sem=recv,
                                         device_id=to, device_id_type=MESH)
        c.start()
        return c

    ev[pl.ds(a * BLK, BLK)] = own[...]
    a_copies = [
        remote(own, ev.at[pl.ds(a * BLK, BLK)], a_send.at[k - 1], a_recv.at[k - 1], ((a + k) % ALPHA, b))
        for k in range(1, ALPHA)
    ]
    v_copies = [
        remote(vall.at[mine], vall.at[mine], v_send.at[k], v_recv.at[k], (a, m)) for k, m in enumerate(mates)
    ]

    for n in (3, 4, 5):
        loads[n].wait()
    for t in range(BLK):
        column = col[t]
        kl = (column >> 7) - q * QUART
        slot = iota((PAIRS, LINKS), 1)
        part = iota((PAIRS, LINKS), 0)
        full = jnp.zeros((PAIRS, LINKS), i32)
        for p in range(PAIRS):
            full = jnp.where(part == p, count[t, p], full)
        kl = jnp.where((slot < full) & (kl >= 0) & (kl < QUART), kl, -1)
        at_rows = slice(t * PAIRS, (t + 1) * PAIRS)
        klq[at_rows, :] = kl.astype(f32)
        u1[at_rows, :] = lcoef[t] * ((128 + (column & 127)) << part).astype(f32)
        u2[at_rows, :] = row[t].astype(f32)
    rank_links(klq, rank)
    kl = klq[...].astype(i32)
    r = rank[...].astype(i32)
    ok = (kl >= 0) & (r < CAP)
    lo[...] = jnp.where(ok, (kl & 3) * CAP + r, -1).astype(f32)
    hi[...] = jnp.where(ok, kl >> 2, -1).astype(f32)
    fl[q] = jnp.broadcast_to(jnp.max(rank[...], keepdims=True), (8, 128))
    f_copies = [
        remote(fl.at[q], fl.at[q], f_send.at[k], f_recv.at[k], (a, m)) for k, m in enumerate(mates)
    ]
    fill_tables(lo, hi, u1, u2, t1, t2)

    for c in a_copies:
        c.wait_recv()
    for t in range(BLK):
        for p in range(PAIRS):
            at[b, t, :, p * ABLK : (p + 1) * ABLK] = ev[src[a * BLK + t, p]]
    y_copies = [
        remote(at.at[b], at.at[b], y_send.at[k], y_recv.at[k], (a, m)) for k, m in enumerate(rings)
    ]
    s_copies = [remote(at.at[b], at.at[b], s_send.at[3], s_recv.at[3], (a, sibling))]

    for c in v_copies:
        c.wait_recv()
    loads[6].wait()
    ints = my_integrals(integ, q * QUART)
    build_coupled(vall, ints, coup, 0, 80)
    for k in (0, 2, 1):
        y_copies[k].wait_recv()
        s_copies.append(
            remote(at.at[back[k]], at.at[back[k]], s_send.at[k], s_recv.at[k], (a, sibling))
        )
    build_coupled(vall, ints, coup, 80, HALF)
    for c in s_copies:
        c.wait_recv()
    keep = pltpu.make_async_copy(at, at_out, o_sem)
    keep.start()

    gather_rows(at, t1, gs)
    pick(coup, gs, ps)
    sums = []
    for t in range(BLK):
        sums.append(add_rows(t2, ps, t).T)
    for k in range(4):
        sb[k] = jnp.concatenate([s[k * SLAB : (k + 1) * SLAB] for s in sums], axis=1)
    for k in range(4):
        rb[4 + k] = sb[k].astype(bf16)
    r_copies = [
        remote(rb.at[4 + (q + k) % 4], rb.at[q], r_send.at[k - 1], r_recv.at[k - 1], (a, mates[k - 1]))
        for k in range(1, 4)
    ]
    total = sb[q]
    for k in range(1, 4):
        r_copies[k - 1].wait_recv()
        total = total + rb[(q + 4 - k) % 4].astype(f32)
    for t in range(BLK):
        out[t * ABLK : (t + 1) * ABLK, :] = total[:, t * ABLK : (t + 1) * ABLK].T
    for c in f_copies:
        c.wait_recv()
    flag_out[...] = jnp.maximum(jnp.maximum(fl[0], fl[1]), jnp.maximum(fl[2], fl[3]))
    keep.wait()
    for c in a_copies + v_copies + f_copies + y_copies + s_copies + r_copies:
        c.wait_send()


def by_links(at, integrals, beta_pair, beta_coef, link_row, link_col, link_coef, link_count):
    blocks = at.transpose(1, 3, 0, 2).reshape(BLK, PAIRS * ABLK, NB)
    pair_hot = (beta_pair[None] == jnp.arange(NP, dtype=i32)[:, None, None]).astype(f32)
    looked_up = jnp.einsum("ki,ibj->kbj", integrals, pair_hot, precision=lax.Precision.HIGHEST)
    coupled = (looked_up * beta_coef[None]).astype(bf16)
    slots = jnp.arange(LINKS, dtype=i32)

    def one(sigma, index):
        t, p = index // PAIRS, index % PAIRS
        column = link_col[t, p]
        amps = jnp.take(blocks[t], p * ABLK + column % ABLK, axis=0)
        rows = jnp.take(coupled, column // ABLK, axis=0)
        picked = jnp.einsum("lbj,lj->lb", rows, amps, preferred_element_type=f32)
        weights = jnp.where(slots < link_count[t, p], link_coef[t, p], 0.0)
        return sigma.at[t * ABLK + link_row[t, p]].add(picked * weights[:, None]), None

    sigma = jnp.zeros((BLK * ABLK, SLAB), f32)
    return lax.scan(one, sigma, jnp.arange(BLK * PAIRS, dtype=i32))[0]


def body(amplitudes, integrals, beta_pair, beta_coef, pair_src, link_row, link_col, link_coef, link_count):
    anym = pl.BlockSpec(memory_space=pl.ANY)
    smem = pl.BlockSpec(memory_space=pltpu.SMEM)
    vmem = pl.BlockSpec(memory_space=pltpu.VMEM)
    rows = pltpu.VMEM((BLK * PAIRS, LINKS), f32)
    dma = pltpu.SemaphoreType.DMA
    sigma, at, most = pl.pallas_call(
        kernel,
        out_shape=(
            jax.ShapeDtypeStruct((BLK * ABLK, SLAB), f32),
            jax.ShapeDtypeStruct((8, BLK, SLAB, PAIRS * ABLK), bf16),
            jax.ShapeDtypeStruct((8, 128), f32),
        ),
        in_specs=[anym, anym, anym, anym, smem, anym, anym, anym, smem],
        out_specs=(vmem, anym, vmem),
        scratch_shapes=[
            pltpu.VMEM((BLK * ABLK, SLAB), bf16),
            pltpu.VMEM((NP, NP), f32),
            pltpu.VMEM((SLAB, NB), i32),
            pltpu.VMEM((SLAB, NB), f32),
            pltpu.VMEM((BLK, PAIRS, LINKS), i32),
            pltpu.VMEM((BLK, PAIRS, LINKS), i32),
            pltpu.VMEM((BLK, PAIRS, LINKS), f32),
            pltpu.VMEM((BLK, SLAB, ABLK), bf16),
            pltpu.VMEM((ALPHA * BLK, SLAB, ABLK), bf16),
            pltpu.VMEM((HALF, NB), f32),
            pltpu.VMEM((8, BLK, SLAB, PAIRS * ABLK), bf16),
            pltpu.VMEM((2, HALF * KROWS, 128), f32),
            rows, rows, rows, rows, rows, rows,
            pltpu.VMEM((BLK, 128, 128), f32),
            pltpu.VMEM((BLK, 32, 128), f32),
            pltpu.VMEM((GROUPS * 4, BLK * CAP, NB), bf16),
            pltpu.VMEM((BLK, GROUPS * 4 * CAP, HALF), bf16),
            pltpu.VMEM((4, SLAB, BLK * ABLK), f32),
            pltpu.VMEM((8, SLAB, BLK * ABLK), bf16),
            pltpu.VMEM((4, 8, 128), f32),
            dma((7,)), dma((15,)), dma((15,)), dma((3,)), dma((3,)), dma((3,)), dma((3,)), dma((4,)),
            dma((4,)), dma((3,)), dma((3,)), dma((3,)), dma((3,)), dma,
        ],
        compiler_params=pltpu.CompilerParams(
            vmem_limit_bytes=48 << 20, collective_id=0, has_side_effects=True
        ),
        name="sigma_links",
    )(amplitudes, integrals, beta_pair, beta_coef, pair_src, link_col, link_row, link_coef, link_count)
    return lax.cond(
        jnp.max(most) >= CAP,
        lambda: by_links(at, integrals, beta_pair, beta_coef, link_row, link_col, link_coef, link_count),
        lambda: sigma,
    )


def solution(mesh):
    in_specs = (P("alpha", "beta"), P(), P("beta", None), P("beta", None), P(),
                P("alpha", None, None), P("alpha", None, None), P("alpha", None, None), P("alpha", None))
    return jax.shard_map(body, mesh=mesh, in_specs=in_specs, out_specs=P("alpha", "beta"), check_vma=False)
```

```python
import jax
import jax.numpy as jnp
from jax import lax
from jax.experimental import pallas as pl
from jax.experimental.pallas import tpu as pltpu
from jax.sharding import PartitionSpec as P

NP = 324
ABLK = 128
LINKS = 1024
PAIRS = 4
BLK = 4
NB = 256
SLAB = 32
ALPHA = 16
HALF = 128
QUART = 81
KROWS = 88
KHIP = 80
FETCH_CAP = 2
CAP = 32
GROUPS = 21
GCHUNK = 7
NTDIMS = (((1,), (1,)), ((), ()))
f32, bf16, i32 = jnp.float32, jnp.bfloat16, jnp.int32
MESH = pl.DeviceIdType.MESH


def dot(a, b):
    return jnp.dot(a, b, preferred_element_type=f32)


def dot_nt(a, b):
    return lax.dot_general(a, b, NTDIMS, preferred_element_type=f32)


def iota(shape, dim):
    return lax.broadcasted_iota(i32, shape, dim)


def hot_bf16(mask):
    return mask.astype(f32).astype(bf16)


def wanted(src, device, owner):
    bits = jnp.int32(0)
    for t in range(BLK):
        for p in range(PAIRS):
            block = src[p, device * BLK + t]
            bits = bits | jnp.where((block >> 2) == owner, bit_of(block & 3), 0)
    return bits


def bit_of(j):
    return jnp.where(j == 0, 1, jnp.where(j == 1, 2, jnp.where(j == 2, 4, 8)))


def lowest(bits):
    return jnp.where(
        (bits & 1) != 0, 0, jnp.where((bits & 2) != 0, 1, jnp.where((bits & 4) != 0, 2, 3))
    )


def my_integrals(integ, first):
    rows = hot_bf16(iota((KROWS, NP), 1) - first == iota((KROWS, NP), 0))
    rows = jnp.where(iota((KROWS, NP), 0) < QUART, rows, jnp.zeros((), bf16))
    mine = dot(rows, integ[...].astype(bf16)).astype(bf16)
    shift = hot_bf16(iota((NP, 128), 0) - 256 == iota((NP, 128), 1))
    return mine[:, :256], dot(mine, shift).astype(bf16)[:, :KHIP]


def build_coupled(v_ref, ints, coup, begin, end):
    lo_ids = iota((256, 256), 0).astype(f32)
    hi_ids = iota((KHIP, 256), 0).astype(f32) + 256.0
    ints_lo, ints_hi = ints

    def one(i, carry):
        v = jnp.concatenate([v_ref[pl.ds(i * 2, 1), :], v_ref[pl.ds(i * 2 + 1, 1), :]], axis=1)
        where_to = jnp.abs(v) - 1.0
        sign = jnp.where(v < 0.0, -1.0, 1.0)
        hot_lo = jnp.where(lo_ids == where_to, sign, 0.0).astype(bf16)
        hot_hi = jnp.where(hi_ids == where_to, sign, 0.0).astype(bf16)
        out = dot(ints_lo, hot_lo) + dot(ints_hi, hot_hi)
        for h in range(2):
            start = pl.multiple_of((i * 2 + h) * KROWS, 8)
            coup[pl.ds(start, KROWS), :] = out[:, h * HALF : (h + 1) * HALF]
        return carry

    lax.fori_loop(begin // 2, end // 2, one, 0, unroll=16)


def rank_links(klq, rank):
    tri = hot_bf16(iota((256, 384), 0) <= iota((256, 384), 1))
    kl_ids = iota((KROWS, 256), 0).astype(f32)

    def one(p, carry):
        carry = list(carry)
        for c in range(4):
            hots = []
            for t in range(BLK):
                row = klq[pl.ds(t * PAIRS + p, 1), c * 256 : (c + 1) * 256]
                hots.append(kl_ids == row)
            stacked = jnp.concatenate([hot_bf16(h) for h in hots], axis=0)
            cum = dot(stacked, tri)
            for t in range(BLK):
                part = cum[t * KROWS : (t + 1) * KROWS]
                base = jnp.concatenate([carry[t], carry[t]], axis=1)
                mine = jnp.where(hots[t], part[:, :256] + base, 0.0)
                got = jnp.sum(mine, axis=0, keepdims=True) - 1.0
                rank[pl.ds(t * PAIRS + p, 1), c * 256 : (c + 1) * 256] = got
                carry[t] = carry[t] + part[:, 256:]
        return tuple(carry)

    zero = jnp.zeros((KROWS, 128), f32)
    lax.fori_loop(0, PAIRS, one, (zero,) * BLK)


def fill_tables(lo, hi, u1, u2, t1, t2):
    lo_ids = iota((128, LINKS), 0).astype(f32)
    hi_ids = iota((32, LINKS), 0).astype(f32)

    def target(t, carry):
        a1 = jnp.zeros((128, 32), f32)
        a2 = jnp.zeros((32, 128), f32)
        for p in range(PAIRS):
            i = t * PAIRS + p
            here = lo_ids == lo[pl.ds(i, 1), :]
            v1 = jnp.where(here, u1[pl.ds(i, 1), :], 0.0).astype(bf16)
            v2 = jnp.where(here, u2[pl.ds(i, 1), :], 0.0).astype(bf16)
            group = hot_bf16(hi_ids == hi[pl.ds(i, 1), :])
            a1 = a1 + dot_nt(v1, group)
            a2 = a2 + dot_nt(group, v2)
        t1[t] = jnp.concatenate([a1, jnp.zeros((128, 96), f32)], axis=1)
        t2[t] = a2
        return carry

    lax.fori_loop(0, BLK, target, 0)


def gather_rows(at, t1, gs, t):
    tables = [((128 + iota((128, 128), 1)) * (1 << p)).astype(f32) for p in range(PAIRS)]
    amps = at[:, t].reshape(HALF, PAIRS * ABLK)
    for c in range(GROUPS // GCHUNK):
        hots = []
        for h in range(GCHUNK):
            code = jnp.take_along_axis(t1[t], jnp.full((128, 128), c * GCHUNK + h, i32), axis=1)
            size = jnp.abs(code)
            sign = jnp.where(code < 0.0, -1.0, 1.0)
            hots.append(
                jnp.concatenate([jnp.where(size == tab, sign, 0.0).astype(bf16) for tab in tables], axis=1)
            )
        rows = dot_nt(jnp.concatenate(hots, axis=0), amps).astype(bf16)
        for h in range(GCHUNK):
            for k in range(4):
                s = h * 128 + k * CAP
                gs[(c * GCHUNK + h) * 4 + k, t * CAP : (t + 1) * CAP, :] = rows[s : s + CAP]


def pick(coup, gs, ps):
    def one(kl, carry):
        c = coup[pl.ds(kl, NB, stride=KROWS), :].astype(bf16)
        q = dot_nt(gs[kl], c).astype(bf16)
        start = pl.multiple_of(kl * CAP, CAP)
        for t in range(BLK):
            ps[t, pl.ds(start, CAP), :] = q[t * CAP : (t + 1) * CAP]
        return carry

    lax.fori_loop(0, QUART, one, 0, unroll=27)
    for t in range(BLK):
        ps[t, QUART * CAP :, :] = jnp.zeros((4 * CAP * GROUPS - QUART * CAP, NB), bf16)


def add_rows(t2, ps, t):
    ids = iota((128, 128), 0).astype(f32)
    hot = jnp.concatenate([hot_bf16(ids == t2[t, g : g + 1, :]) for g in range(GROUPS)], axis=1)
    return dot(hot, ps[t])


def kernel(amp_h, integ_h, pair_h, coef_h, src_h, col_h, row_h, lcoef_h, count_h, out, flag_out,
           src, count, amp, blocks, give, integ, pair, coef, col, row, lcoef, ev, vown, vall, at, coup, klq, rank, lo, hi, u1, u2,
           t1, t2, gs, ps, sb, rb, fl, in_sem, a_send, a_recv, v_send, v_recv, y_send, y_recv, s_send,
           s_recv, r_send, r_recv, f_send, f_recv, g_send, g_recv):
    a, b = lax.axis_index("alpha"), lax.axis_index("beta")
    core = b % 2
    half, q = b // 4, b % 4
    x, z = a // 4, a % 4
    sibling = b // 2 * 2 + 1 - core
    across = half * 4 + (q + 2) % 4
    peers = [(b + k) % 8 for k in range(1, 8)]

    loads = []
    for n, (h, m) in enumerate([(amp_h, amp), (pair_h, pair), (coef_h, coef), (col_h, col), (row_h, row),
                                (lcoef_h, lcoef), (integ_h, integ), (src_h, src),
                                (count_h, count)]):
        loads.append(pltpu.make_async_copy(h, m, in_sem.at[n]))
        loads[-1].start()

    barrier = pltpu.get_barrier_semaphore()
    for k in range(1, ALPHA):
        pl.semaphore_signal(barrier, inc=1, device_id=((a + k) % ALPHA, b), device_id_type=MESH)
    for k in range(1, 8):
        pl.semaphore_signal(barrier, inc=1, device_id=(a, (b + k) % 8), device_id_type=MESH)

    loads[0].wait()
    loads[7].wait()
    for j in range(BLK):
        blocks[j] = amp[:, j * ABLK : (j + 1) * ABLK]
    for k in range(ALPHA):
        asked = wanted(src, (a + k) % ALPHA, a)
        low = lowest(asked)
        for n, j in enumerate((low, lowest(asked - bit_of(low)))):
            give[k, n] = blocks[j]
    ev[pl.ds(a * FETCH_CAP, FETCH_CAP)] = give[0]
    pl.semaphore_wait(barrier, ALPHA - 1 + 7)

    def remote(source, target, send, recv, to):
        c = pltpu.make_async_remote_copy(src_ref=source, dst_ref=target, send_sem=send, recv_sem=recv,
                                         device_id=to, device_id_type=MESH)
        c.start()
        return c

    a_copies = [
        remote(give.at[k], ev.at[pl.ds(a * FETCH_CAP, FETCH_CAP)], a_send.at[k - 1], a_recv.at[k - 1], ((a + k) % ALPHA, b))
        for k in range(1, ALPHA)
    ]
    loads[1].wait()
    loads[2].wait()
    mine = pl.ds(pl.multiple_of(b * SLAB, SLAB), SLAB)
    codes = coef[...] * (pair[...] + 1).astype(f32)
    for h in range(2):
        vown[h] = codes[:, h * HALF : (h + 1) * HALF]
    vall[mine, :] = vown[half]
    v_copies = [
        remote(vown.at[m // 4], vall.at[mine], v_send.at[k], v_recv.at[k], (a, m)) for k, m in enumerate(peers)
    ]

    for n in (3, 4, 5, 8):
        loads[n].wait()
    for t in range(BLK):
        column = col[t]
        kl = (column >> 7) - q * QUART
        slot = iota((PAIRS, LINKS), 1)
        part = iota((PAIRS, LINKS), 0)
        full = jnp.zeros((PAIRS, LINKS), i32)
        for p in range(PAIRS):
            full = jnp.where(part == p, count[t, p], full)
        kl = jnp.where((slot < full) & (kl >= 0) & (kl < QUART), kl, -1)
        at_rows = slice(t * PAIRS, (t + 1) * PAIRS)
        klq[at_rows, :] = kl.astype(f32)
        u1[at_rows, :] = lcoef[t] * ((128 + (column & 127)) << part).astype(f32)
        u2[at_rows, :] = row[t].astype(f32)
    rank_links(klq, rank)
    kl = klq[...].astype(i32)
    r = rank[...].astype(i32)
    ok = (kl >= 0) & (r < CAP)
    lo[...] = jnp.where(ok, (kl & 3) * CAP + r, -1).astype(f32)
    hi[...] = jnp.where(ok, kl >> 2, -1).astype(f32)
    fl[b] = jnp.broadcast_to(jnp.max(rank[...], keepdims=True), (8, 128))
    f_copies = [
        remote(fl.at[b], fl.at[b], f_send.at[k], f_recv.at[k], (a, m)) for k, m in enumerate(peers)
    ]
    fill_tables(lo, hi, u1, u2, t1, t2)

    for c in a_copies:
        c.wait_recv()
    y_copies, s_copies = [], []
    for t in range(BLK):
        for p in range(PAIRS):
            block = src[p, a * BLK + t]
            owner = block >> 2
            below = wanted(src, a, owner) & (bit_of(block & 3) - 1)
            at[q, t, :, p * ABLK : (p + 1) * ABLK] = ev[
                owner * FETCH_CAP + jnp.where(below != 0, 1, 0)
            ]
        mine = at.at[q, t]
        y_copies.append(remote(mine, mine, y_send.at[t], y_recv.at[t], (a, across)))
        s_copies.append([remote(mine, mine, s_send.at[t, 0], s_recv.at[t, 0], (a, sibling))])

    for c in v_copies:
        c.wait_recv()
    loads[6].wait()
    ints = my_integrals(integ, q * QUART)
    for c in f_copies:
        c.wait_recv()
    most = fl[0]
    for k in range(1, 8):
        most = jnp.maximum(most, fl[k])
    fl[8] = most
    g_copies = [
        remote(fl.at[8], fl.at[8 + k], g_send.at[k - 1], g_recv.at[k - 1], (x * 4 + (z + k) % 4, b))
        for k in range(1, 4)
    ]
    for t in range(BLK):
        build_coupled(vall, ints, coup, t * 64, t * 64 + 64)
        y_copies[t].wait_recv()
        away = at.at[(q + 2) % 4, t]
        s_copies[t].append(remote(away, away, s_send.at[t, 1], s_recv.at[t, 1], (a, sibling)))
    for c in g_copies:
        c.wait_recv()
    fl[12] = jnp.maximum(jnp.maximum(fl[8], fl[9]), jnp.maximum(fl[10], fl[11]))
    g_copies += [
        remote(fl.at[12], fl.at[12 + k], g_send.at[2 + k], g_recv.at[2 + k], ((x + k) % 4 * 4 + z, b))
        for k in range(1, 4)
    ]
    for t in range(BLK):
        for c in s_copies[t]:
            c.wait_recv()
        gather_rows(at, t1, gs, t)
    pick(coup, gs, ps)
    r_copies = []
    for t in range(BLK):
        part = add_rows(t2, ps, t).T
        for k in range(8):
            slab = part[k * SLAB : (k + 1) * SLAB]
            sb[t, k] = slab
            rb[t, 8 + k] = slab.astype(bf16)
        r_copies.append([
            remote(rb.at[t, 8 + m], rb.at[t, b], r_send.at[t, k], r_recv.at[t, k], (a, m))
            for k, m in enumerate(peers)
        ])
    for t in range(BLK):
        total = sb[t, b]
        for k in range(1, 8):
            r_copies[t][k - 1].wait_recv()
            total = total + rb[t, (b + 8 - k) % 8].astype(f32)
        out[:, t * ABLK : (t + 1) * ABLK] = total
    for c in g_copies[3:]:
        c.wait_recv()
    flag_out[0] = jnp.max(fl[12:16])
    for c in a_copies + v_copies + f_copies + g_copies + y_copies + sum(s_copies + r_copies, []):
        c.wait_send()


def assemble(local_amp, pair_src, num_local):
    alpha_count = lax.axis_size("alpha")
    my_index = lax.axis_index("alpha")
    block_total = pair_src.shape[0]
    block_rows = local_amp.shape[1]
    slab_width = local_amp.shape[2]
    my_requests = lax.dynamic_slice_in_dim(pair_src, my_index * num_local, num_local, 0)
    owned_ids = my_index * num_local + jnp.arange(num_local, dtype=jnp.int32)
    requests = pair_src.reshape(alpha_count, -1)
    asked_for = jnp.any(requests[:, :, None] == owned_ids[None, None, :], axis=1)
    position = jnp.cumsum(asked_for.astype(jnp.int32), axis=1) - 1
    slot_ids = jnp.arange(FETCH_CAP, dtype=jnp.int32)
    select = (asked_for[:, None, :] & (position[:, None, :] == slot_ids[None, :, None])).astype(
        local_amp.dtype
    )
    outgoing = jnp.einsum(
        "qsj,jab->qsab", select, local_amp, preferred_element_type=jnp.float32
    ).astype(local_amp.dtype)
    incoming = lax.all_to_all(outgoing, "alpha", split_axis=0, concat_axis=0, tiled=True)
    combined = jnp.concatenate([local_amp, incoming.reshape(-1, block_rows, slab_width)], axis=0)
    catalog = jnp.arange(block_total, dtype=jnp.int32).reshape(alpha_count, num_local)
    wanted = jnp.any(my_requests.reshape(-1)[:, None, None] == catalog[None], axis=0)
    order_pos = jnp.cumsum(wanted.astype(jnp.int32), axis=1) - 1
    owner_dev = my_requests // num_local
    within = my_requests % num_local
    remote = num_local + owner_dev * FETCH_CAP + order_pos[owner_dev, within]
    return (combined, jnp.where(owner_dev == my_index, within, remote))


def by_links(
    amplitudes, integrals, beta_pair, beta_coef, pair_src, link_row, link_col, link_coef, link_count
):
    num_local = link_row.shape[0]
    slab_piece = amplitudes.shape[1]
    local_amp = amplitudes.reshape(num_local, ABLK, slab_piece)
    full_rows = lax.all_gather(local_amp, "beta", axis=2, tiled=True)
    gathered, sources = assemble(full_rows, pair_src, num_local)
    pair_ids = jnp.arange(NP, dtype=jnp.int32)
    pair_hot = (beta_pair[None, :, :] == pair_ids[:, None, None]).astype(jnp.float32)
    looked_up = jnp.einsum("ki,ibj->kbj", integrals, pair_hot, precision=lax.Precision.HIGHEST)
    coupled = (looked_up * beta_coef[None]).astype(jnp.bfloat16)
    link_ids = jnp.arange(LINKS, dtype=jnp.int32)
    string_ids = jnp.arange(ABLK, dtype=jnp.int32)

    def per_target(target, sigma_acc):
        chosen = lax.dynamic_index_in_dim(sources, target, 0, keepdims=False)
        columns = lax.dynamic_index_in_dim(link_col, target, 0, keepdims=False)
        occupied = lax.dynamic_index_in_dim(link_count, target, 0, keepdims=False)
        signs = lax.dynamic_index_in_dim(link_coef, target, 0, keepdims=False)
        targets_row = lax.dynamic_index_in_dim(link_row, target, 0, keepdims=False)

        def per_pair(total, pair_index):
            block = jnp.take(gathered, chosen[pair_index], axis=0)
            column_row = columns[pair_index]
            orbital_pair = column_row // ABLK
            source_row = column_row % ABLK
            amp_rows = jnp.take(block, source_row, axis=0)
            coupled_rows = jnp.take(coupled, orbital_pair, axis=0)
            picked = jnp.einsum(
                "lbj,lj->lb", coupled_rows, amp_rows, preferred_element_type=jnp.float32
            )
            weights = jnp.where(
                link_ids < occupied[pair_index], signs[pair_index], jnp.float32(0.0)
            )
            hot_rows = (targets_row[pair_index][:, None] == string_ids[None, :]).astype(jnp.float32)
            added = jnp.dot(
                hot_rows.T,
                picked * weights[:, None],
                precision=lax.Precision.HIGHEST,
                preferred_element_type=jnp.float32,
            )
            return (total + added, None)

        start = jnp.zeros((ABLK, slab_piece), jnp.float32)
        result, unused = lax.scan(per_pair, start, jnp.arange(chosen.shape[0], dtype=jnp.int32))
        return lax.dynamic_update_index_in_dim(sigma_acc, result, target, 0)

    sigma_acc = jnp.zeros((num_local, ABLK, slab_piece), jnp.float32)
    sigma_acc = lax.fori_loop(0, num_local, per_target, sigma_acc)
    return sigma_acc.reshape(num_local * ABLK, slab_piece)


def body(amplitudes, integrals, beta_pair, beta_coef, pair_src, link_row, link_col, link_coef, link_count):
    anym = pl.BlockSpec(memory_space=pl.ANY)
    smem = pl.BlockSpec(memory_space=pltpu.SMEM)
    vmem = pl.BlockSpec(memory_space=pltpu.VMEM)
    rows = pltpu.VMEM((BLK * PAIRS, LINKS), f32)
    dma = pltpu.SemaphoreType.DMA
    sigma, most = pl.pallas_call(
        kernel,
        out_shape=(
            jax.ShapeDtypeStruct((SLAB, BLK * ABLK), f32),
            jax.ShapeDtypeStruct((1,), f32),
        ),
        in_specs=[anym] * 9,
        out_specs=(vmem, smem),
        scratch_shapes=[
            pltpu.SMEM((PAIRS, ALPHA * BLK), i32),
            pltpu.SMEM((BLK, PAIRS), i32),
            pltpu.VMEM((SLAB, BLK * ABLK), bf16),
            pltpu.VMEM((BLK, SLAB, ABLK), bf16),
            pltpu.VMEM((ALPHA, FETCH_CAP, SLAB, ABLK), bf16),
            pltpu.VMEM((NP, NP), f32),
            pltpu.VMEM((SLAB, NB), i32),
            pltpu.VMEM((SLAB, NB), f32),
            pltpu.VMEM((BLK, PAIRS, LINKS), i32),
            pltpu.VMEM((BLK, PAIRS, LINKS), i32),
            pltpu.VMEM((BLK, PAIRS, LINKS), f32),
            pltpu.VMEM((ALPHA * FETCH_CAP, SLAB, ABLK), bf16),
            pltpu.VMEM((2, SLAB, HALF), f32),
            pltpu.VMEM((NB, HALF), f32),
            pltpu.VMEM((4, BLK, SLAB, PAIRS * ABLK), bf16),
            pltpu.VMEM((NB * KROWS, HALF), f32),
            rows, rows, rows, rows, rows, rows,
            pltpu.VMEM((BLK, 128, 128), f32),
            pltpu.VMEM((BLK, 32, 128), f32),
            pltpu.VMEM((GROUPS * 4, BLK * CAP, HALF), bf16),
            pltpu.VMEM((BLK, GROUPS * 4 * CAP, NB), bf16),
            pltpu.VMEM((BLK, 8, SLAB, ABLK), f32),
            pltpu.VMEM((BLK, 16, SLAB, ABLK), bf16),
            pltpu.VMEM((16, 8, 128), f32),
            dma((9,)), dma((15,)), dma((15,)), dma((7,)), dma((7,)), dma((BLK,)), dma((BLK,)),
            dma((BLK, 2)), dma((BLK, 2)), dma((BLK, 7)), dma((BLK, 7)), dma((7,)), dma((7,)), dma((6,)), dma((6,)),
        ],
        compiler_params=pltpu.CompilerParams(
            vmem_limit_bytes=60 << 20, collective_id=0, has_side_effects=True
        ),
        name="sigma_links",
    )(amplitudes.T, integrals, beta_pair, beta_coef, pair_src.T, link_col, link_row, link_coef, link_count)
    out = lax.cond(
        most[0] >= CAP,
        lambda: by_links(amplitudes, integrals, beta_pair, beta_coef, pair_src, link_row, link_col, link_coef,
                         link_count).T,
        lambda: sigma,
    )
    return out.T


def solution(mesh):
    in_specs = (P("alpha", "beta"), P(), P("beta", None), P("beta", None), P(),
                P("alpha", None, None), P("alpha", None, None), P("alpha", None, None), P("alpha", None))
    return jax.shard_map(body, mesh=mesh, in_specs=in_specs, out_specs=P("alpha", "beta"), check_vma=False)
```

```python
import jax
import jax.numpy as jnp
from jax import lax
from jax.experimental import pallas as pl
from jax.experimental.pallas import tpu as pltpu
from jax.sharding import PartitionSpec as P

NP = 324
ABLK = 128
LINKS = 1024
PAIRS = 4
BLK = 4
NB = 256
SLAB = 32
ALPHA = 16
HALF = 128
QUART = 81
KROWS = 88
KHIP = 80
FETCH_CAP = 2
CAP = 32
GROUPS = 21
GCHUNK = 7
CHUNKS = 2
SPAN = BLK // CHUNKS
NTDIMS = (((1,), (1,)), ((), ()))
f32, bf16, i32 = jnp.float32, jnp.bfloat16, jnp.int32
MESH = pl.DeviceIdType.MESH


def dot(a, b):
    return jnp.dot(a, b, preferred_element_type=f32)


def dot_nt(a, b):
    return lax.dot_general(a, b, NTDIMS, preferred_element_type=f32)


def iota(shape, dim):
    return lax.broadcasted_iota(i32, shape, dim)


def hot_bf16(mask):
    return mask.astype(f32).astype(bf16)


def wanted(src, device, owner):
    bits = jnp.int32(0)
    for t in range(BLK):
        for p in range(PAIRS):
            block = src[p, device * BLK + t]
            bits = bits | jnp.where((block >> 2) == owner, bit_of(block & 3), 0)
    return bits


def bit_of(j):
    return jnp.where(j == 0, 1, jnp.where(j == 1, 2, jnp.where(j == 2, 4, 8)))


def lowest(bits):
    return jnp.where(
        (bits & 1) != 0, 0, jnp.where((bits & 2) != 0, 1, jnp.where((bits & 4) != 0, 2, 3))
    )


def my_integrals(integ, first):
    rows = hot_bf16(iota((KROWS, NP), 1) - first == iota((KROWS, NP), 0))
    rows = jnp.where(iota((KROWS, NP), 0) < QUART, rows, jnp.zeros((), bf16))
    mine = dot(rows, integ[...].astype(bf16)).astype(bf16)
    shift = hot_bf16(iota((NP, 128), 0) - 256 == iota((NP, 128), 1))
    return mine[:, :256], dot(mine, shift).astype(bf16)[:, :KHIP]


def build_coupled(v_ref, ints, coup, begin, end):
    lo_ids = iota((256, 256), 0).astype(f32)
    hi_ids = iota((KHIP, 256), 0).astype(f32) + 256.0
    ints_lo, ints_hi = ints

    def one(i, carry):
        v = jnp.concatenate([v_ref[pl.ds(i * 2, 1), :], v_ref[pl.ds(i * 2 + 1, 1), :]], axis=1)
        where_to = jnp.abs(v) - 1.0
        sign = jnp.where(v < 0.0, -1.0, 1.0)
        hot_lo = jnp.where(lo_ids == where_to, sign, 0.0).astype(bf16)
        hot_hi = jnp.where(hi_ids == where_to, sign, 0.0).astype(bf16)
        out = dot(ints_lo, hot_lo) + dot(ints_hi, hot_hi)
        for h in range(2):
            start = pl.multiple_of((i * 2 + h) * KROWS, 8)
            coup[pl.ds(start, KROWS), :] = out[:, h * HALF : (h + 1) * HALF]
        return carry

    lax.fori_loop(begin // 2, end // 2, one, 0, unroll=16)


def rank_links(klq, rank):
    tri = hot_bf16(iota((256, 384), 0) <= iota((256, 384), 1))
    kl_ids = iota((KROWS, 256), 0).astype(f32)

    def one(p, carry):
        carry = list(carry)
        for c in range(4):
            hots = []
            for t in range(BLK):
                row = klq[pl.ds(t * PAIRS + p, 1), c * 256 : (c + 1) * 256]
                hots.append(kl_ids == row)
            stacked = jnp.concatenate([hot_bf16(h) for h in hots], axis=0)
            cum = dot(stacked, tri)
            for t in range(BLK):
                part = cum[t * KROWS : (t + 1) * KROWS]
                base = jnp.concatenate([carry[t], carry[t]], axis=1)
                mine = jnp.where(hots[t], part[:, :256] + base, 0.0)
                got = jnp.sum(mine, axis=0, keepdims=True) - 1.0
                rank[pl.ds(t * PAIRS + p, 1), c * 256 : (c + 1) * 256] = got
                carry[t] = carry[t] + part[:, 256:]
        return tuple(carry)

    zero = jnp.zeros((KROWS, 128), f32)
    lax.fori_loop(0, PAIRS, one, (zero,) * BLK, unroll=2)


def fill_tables(lo, hi, u1, u2, t1, t2):
    lo_ids = iota((128, LINKS), 0).astype(f32)
    hi_ids = iota((32, LINKS), 0).astype(f32)

    def target(t, carry):
        a1 = jnp.zeros((128, 32), f32)
        a2 = jnp.zeros((32, 128), f32)
        for p in range(PAIRS):
            i = t * PAIRS + p
            here = lo_ids == lo[pl.ds(i, 1), :]
            v1 = jnp.where(here, u1[pl.ds(i, 1), :], 0.0).astype(bf16)
            v2 = jnp.where(here, u2[pl.ds(i, 1), :], 0.0).astype(bf16)
            group = hot_bf16(hi_ids == hi[pl.ds(i, 1), :])
            a1 = a1 + dot_nt(v1, group)
            a2 = a2 + dot_nt(group, v2)
        t1[t] = jnp.concatenate([a1, jnp.zeros((128, 96), f32)], axis=1)
        t2[t] = a2
        return carry

    lax.fori_loop(0, BLK, target, 0, unroll=2)


def gather_rows(at, t1, gs, t):
    tables = [((128 + iota((128, 128), 1)) * (1 << p)).astype(f32) for p in range(PAIRS)]
    amps = at[:, t].reshape(HALF, PAIRS * ABLK)
    for c in range(GROUPS // GCHUNK):
        hots = []
        for h in range(GCHUNK):
            code = jnp.take_along_axis(t1[t], jnp.full((128, 128), c * GCHUNK + h, i32), axis=1)
            size = jnp.abs(code)
            sign = jnp.where(code < 0.0, -1.0, 1.0)
            hots.append(
                jnp.concatenate([jnp.where(size == tab, sign, 0.0).astype(bf16) for tab in tables], axis=1)
            )
        rows = dot_nt(jnp.concatenate(hots, axis=0), amps).astype(bf16)
        for h in range(GCHUNK):
            for k in range(4):
                s = h * 128 + k * CAP
                gs[(c * GCHUNK + h) * 4 + k, t * CAP : (t + 1) * CAP, :] = rows[s : s + CAP]


def pick(coup, gs, ps):
    def one(kl, carry):
        c = coup[pl.ds(kl, NB, stride=KROWS), :].astype(bf16)
        q = dot_nt(gs[kl], c).astype(bf16)
        start = pl.multiple_of(kl * CAP, CAP)
        for t in range(BLK):
            ps[t, pl.ds(start, CAP), :] = q[t * CAP : (t + 1) * CAP]
        return carry

    lax.fori_loop(0, QUART, one, 0, unroll=27)
    for t in range(BLK):
        ps[t, QUART * CAP :, :] = jnp.zeros((4 * CAP * GROUPS - QUART * CAP, NB), bf16)


def add_rows(t2, ps, t):
    ids = iota((128, 128), 0).astype(f32)
    hot = jnp.concatenate([hot_bf16(ids == t2[t, g : g + 1, :]) for g in range(GROUPS)], axis=1)
    return dot(hot, ps[t])


def kernel(amp_h, integ_h, pair_h, coef_h, src_h, col_h, row_h, lcoef_h, count_h, out, flag_out,
           src, count, amp, blocks, give, integ, pair, coef, col, row, lcoef, ev, vown, vall, at, coup, klq, rank, lo, hi, u1, u2,
           t1, t2, gs, ps, sb, rb, fl, in_sem, a_send, a_recv, v_send, v_recv, y_send, y_recv, s_send,
           s_recv, r_send, r_recv, f_send, f_recv, g_send, g_recv):
    a, b = lax.axis_index("alpha"), lax.axis_index("beta")
    core = b % 2
    half, q = b // 4, b % 4
    x, z = a // 4, a % 4
    sibling = b // 2 * 2 + 1 - core
    across = half * 4 + (q + 2) % 4
    peers = [(b + k) % 8 for k in range(1, 8)]
    mates = [half * 4 + (q + k) % 4 for k in range(1, 4)]

    loads = []
    for n, (h, m) in enumerate([(amp_h, amp), (pair_h, pair), (coef_h, coef), (col_h, col), (row_h, row),
                                (lcoef_h, lcoef), (integ_h, integ), (src_h, src),
                                (count_h, count)]):
        loads.append(pltpu.make_async_copy(h, m, in_sem.at[n]))
        loads[-1].start()

    barrier = pltpu.get_barrier_semaphore()
    for k in range(1, ALPHA):
        pl.semaphore_signal(barrier, inc=1, device_id=((a + k) % ALPHA, b), device_id_type=MESH)
    for k in range(1, 8):
        pl.semaphore_signal(barrier, inc=1, device_id=(a, (b + k) % 8), device_id_type=MESH)

    loads[0].wait()
    loads[7].wait()
    for j in range(BLK):
        blocks[j] = amp[:, j * ABLK : (j + 1) * ABLK]
    for k in range(ALPHA):
        asked = wanted(src, (a + k) % ALPHA, a)
        low = lowest(asked)
        for n, j in enumerate((low, lowest(asked - bit_of(low)))):
            give[k, n] = blocks[j]
    ev[pl.ds(a * FETCH_CAP, FETCH_CAP)] = give[0]
    pl.semaphore_wait(barrier, ALPHA - 1 + 7)

    def remote(source, target, send, recv, to):
        c = pltpu.make_async_remote_copy(src_ref=source, dst_ref=target, send_sem=send, recv_sem=recv,
                                         device_id=to, device_id_type=MESH)
        c.start()
        return c

    a_copies = [
        remote(give.at[k], ev.at[pl.ds(a * FETCH_CAP, FETCH_CAP)], a_send.at[k - 1], a_recv.at[k - 1], ((a + k) % ALPHA, b))
        for k in range(1, ALPHA)
    ]
    loads[1].wait()
    loads[2].wait()
    mine = pl.ds(pl.multiple_of(b * SLAB, SLAB), SLAB)
    codes = coef[...] * (pair[...] + 1).astype(f32)
    for h in range(2):
        vown[h] = codes[:, h * HALF : (h + 1) * HALF]
    vall[mine, :] = vown[half]
    v_copies = [
        remote(vown.at[m // 4], vall.at[mine], v_send.at[k], v_recv.at[k], (a, m)) for k, m in enumerate(peers)
    ]

    for n in (3, 4, 5, 8):
        loads[n].wait()
    for t in range(BLK):
        column = col[t]
        kl = (column >> 7) - q * QUART
        slot = iota((PAIRS, LINKS), 1)
        part = iota((PAIRS, LINKS), 0)
        full = jnp.zeros((PAIRS, LINKS), i32)
        for p in range(PAIRS):
            full = jnp.where(part == p, count[t, p], full)
        kl = jnp.where((slot < full) & (kl >= 0) & (kl < QUART), kl, -1)
        at_rows = slice(t * PAIRS, (t + 1) * PAIRS)
        klq[at_rows, :] = kl.astype(f32)
        u1[at_rows, :] = lcoef[t] * ((128 + (column & 127)) << part).astype(f32)
        u2[at_rows, :] = row[t].astype(f32)
    rank_links(klq, rank)
    kl = klq[...].astype(i32)
    r = rank[...].astype(i32)
    ok = (kl >= 0) & (r < CAP)
    lo[...] = jnp.where(ok, (kl & 3) * CAP + r, -1).astype(f32)
    hi[...] = jnp.where(ok, kl >> 2, -1).astype(f32)
    fl[q] = jnp.broadcast_to(jnp.max(rank[...], keepdims=True), (8, 128))
    f_copies = [
        remote(fl.at[q], fl.at[q], f_send.at[k], f_recv.at[k], (a, m)) for k, m in enumerate(mates)
    ]
    fill_tables(lo, hi, u1, u2, t1, t2)

    for c in a_copies:
        c.wait_recv()
    y_copies, s_copies = [], []
    for t in range(BLK):
        for p in range(PAIRS):
            block = src[p, a * BLK + t]
            owner = block >> 2
            below = wanted(src, a, owner) & (bit_of(block & 3) - 1)
            at[q, t, :, p * ABLK : (p + 1) * ABLK] = ev[
                owner * FETCH_CAP + jnp.where(below != 0, 1, 0)
            ]
        if t % 2:
            pair = pl.ds(t - 1, 2)
            mine, n = at.at[q, pair], t // 2
            y_copies.append(remote(mine, mine, y_send.at[n], y_recv.at[n], (a, across)))
            s_copies.append([remote(mine, mine, s_send.at[n, 0], s_recv.at[n, 0], (a, sibling))])

    for c in v_copies:
        c.wait_recv()
    loads[6].wait()
    ints = my_integrals(integ, q * QUART)
    for c in f_copies:
        c.wait_recv()
    fl[8] = jnp.maximum(jnp.maximum(fl[0], fl[1]), jnp.maximum(fl[2], fl[3]))
    g_copies = [
        remote(fl.at[8], fl.at[8 + k], g_send.at[k - 1], g_recv.at[k - 1], (x * 4 + (z + k) % 4, b))
        for k in range(1, 4)
    ]
    for t in range(BLK):
        build_coupled(vall, ints, coup, t * 64, t * 64 + 64)
        if t in (1, 2):
            y_copies[t - 1].wait_recv()
            away = at.at[(q + 2) % 4, pl.ds(t * 2 - 2, 2)]
            s_copies[t - 1].append(
                remote(away, away, s_send.at[t - 1, 1], s_recv.at[t - 1, 1], (a, sibling))
            )
    for c in g_copies:
        c.wait_recv()
    fl[12] = jnp.maximum(jnp.maximum(fl[8], fl[9]), jnp.maximum(fl[10], fl[11]))
    g_copies += [
        remote(fl.at[12], fl.at[12 + k], g_send.at[2 + k], g_recv.at[2 + k], ((x + k) % 4 * 4 + z, b))
        for k in range(1, 4)
    ]
    for t in range(BLK):
        if t % 2 == 0:
            for c in s_copies[t // 2]:
                c.wait_recv()
        gather_rows(at, t1, gs, t)
    pick(coup, gs, ps)
    r_copies = []
    for n in range(CHUNKS):
        parts = [add_rows(t2, ps, n * SPAN + i).T for i in range(SPAN)]
        for k in range(8):
            slab = jnp.concatenate([part[k * SLAB : (k + 1) * SLAB] for part in parts], axis=1)
            sb[n, k] = slab
            rb[n, 8 + k] = slab.astype(bf16)
        r_copies.append([
            remote(rb.at[n, 8 + peers[k]], rb.at[n, b], r_send.at[n, k], r_recv.at[n, k], (a, peers[k]))
            for k in (3, 2, 4, 1, 5, 0, 6)
        ])
    for c in a_copies + v_copies + f_copies + g_copies + y_copies + sum(s_copies, []):
        c.wait_send()
    for n in range(CHUNKS):
        for c in r_copies[n]:
            c.wait_recv()
        total = sb[n, b]
        for k in range(1, 8):
            total = total + rb[n, (b + 8 - k) % 8].astype(f32)
        out[:, n * SPAN * ABLK : (n + 1) * SPAN * ABLK] = total
    for c in g_copies[3:]:
        c.wait_recv()
    flag_out[0] = jnp.max(fl[12:16])
    for c in sum(r_copies, []):
        c.wait_send()


def assemble(local_amp, pair_src, num_local):
    alpha_count = lax.axis_size("alpha")
    my_index = lax.axis_index("alpha")
    block_total = pair_src.shape[0]
    block_rows = local_amp.shape[1]
    slab_width = local_amp.shape[2]
    my_requests = lax.dynamic_slice_in_dim(pair_src, my_index * num_local, num_local, 0)
    owned_ids = my_index * num_local + jnp.arange(num_local, dtype=jnp.int32)
    requests = pair_src.reshape(alpha_count, -1)
    asked_for = jnp.any(requests[:, :, None] == owned_ids[None, None, :], axis=1)
    position = jnp.cumsum(asked_for.astype(jnp.int32), axis=1) - 1
    slot_ids = jnp.arange(FETCH_CAP, dtype=jnp.int32)
    select = (asked_for[:, None, :] & (position[:, None, :] == slot_ids[None, :, None])).astype(
        local_amp.dtype
    )
    outgoing = jnp.einsum(
        "qsj,jab->qsab", select, local_amp, preferred_element_type=jnp.float32
    ).astype(local_amp.dtype)
    incoming = lax.all_to_all(outgoing, "alpha", split_axis=0, concat_axis=0, tiled=True)
    combined = jnp.concatenate([local_amp, incoming.reshape(-1, block_rows, slab_width)], axis=0)
    catalog = jnp.arange(block_total, dtype=jnp.int32).reshape(alpha_count, num_local)
    wanted = jnp.any(my_requests.reshape(-1)[:, None, None] == catalog[None], axis=0)
    order_pos = jnp.cumsum(wanted.astype(jnp.int32), axis=1) - 1
    owner_dev = my_requests // num_local
    within = my_requests % num_local
    remote = num_local + owner_dev * FETCH_CAP + order_pos[owner_dev, within]
    return (combined, jnp.where(owner_dev == my_index, within, remote))


def by_links(
    amplitudes, integrals, beta_pair, beta_coef, pair_src, link_row, link_col, link_coef, link_count
):
    num_local = link_row.shape[0]
    slab_piece = amplitudes.shape[1]
    local_amp = amplitudes.reshape(num_local, ABLK, slab_piece)
    full_rows = lax.all_gather(local_amp, "beta", axis=2, tiled=True)
    gathered, sources = assemble(full_rows, pair_src, num_local)
    pair_ids = jnp.arange(NP, dtype=jnp.int32)
    pair_hot = (beta_pair[None, :, :] == pair_ids[:, None, None]).astype(jnp.float32)
    looked_up = jnp.einsum("ki,ibj->kbj", integrals, pair_hot, precision=lax.Precision.HIGHEST)
    coupled = (looked_up * beta_coef[None]).astype(jnp.bfloat16)
    link_ids = jnp.arange(LINKS, dtype=jnp.int32)
    string_ids = jnp.arange(ABLK, dtype=jnp.int32)

    def per_target(target, sigma_acc):
        chosen = lax.dynamic_index_in_dim(sources, target, 0, keepdims=False)
        columns = lax.dynamic_index_in_dim(link_col, target, 0, keepdims=False)
        occupied = lax.dynamic_index_in_dim(link_count, target, 0, keepdims=False)
        signs = lax.dynamic_index_in_dim(link_coef, target, 0, keepdims=False)
        targets_row = lax.dynamic_index_in_dim(link_row, target, 0, keepdims=False)

        def per_pair(total, pair_index):
            block = jnp.take(gathered, chosen[pair_index], axis=0)
            column_row = columns[pair_index]
            orbital_pair = column_row // ABLK
            source_row = column_row % ABLK
            amp_rows = jnp.take(block, source_row, axis=0)
            coupled_rows = jnp.take(coupled, orbital_pair, axis=0)
            picked = jnp.einsum(
                "lbj,lj->lb", coupled_rows, amp_rows, preferred_element_type=jnp.float32
            )
            weights = jnp.where(
                link_ids < occupied[pair_index], signs[pair_index], jnp.float32(0.0)
            )
            hot_rows = (targets_row[pair_index][:, None] == string_ids[None, :]).astype(jnp.float32)
            added = jnp.dot(
                hot_rows.T,
                picked * weights[:, None],
                precision=lax.Precision.HIGHEST,
                preferred_element_type=jnp.float32,
            )
            return (total + added, None)

        start = jnp.zeros((ABLK, slab_piece), jnp.float32)
        result, unused = lax.scan(per_pair, start, jnp.arange(chosen.shape[0], dtype=jnp.int32))
        return lax.dynamic_update_index_in_dim(sigma_acc, result, target, 0)

    sigma_acc = jnp.zeros((num_local, ABLK, slab_piece), jnp.float32)
    sigma_acc = lax.fori_loop(0, num_local, per_target, sigma_acc)
    return sigma_acc.reshape(num_local * ABLK, slab_piece)


def body(amplitudes, integrals, beta_pair, beta_coef, pair_src, link_row, link_col, link_coef, link_count):
    anym = pl.BlockSpec(memory_space=pl.ANY)
    smem = pl.BlockSpec(memory_space=pltpu.SMEM)
    vmem = pl.BlockSpec(memory_space=pltpu.VMEM)
    rows = pltpu.VMEM((BLK * PAIRS, LINKS), f32)
    dma = pltpu.SemaphoreType.DMA
    sigma, most = pl.pallas_call(
        kernel,
        out_shape=(
            jax.ShapeDtypeStruct((SLAB, BLK * ABLK), f32),
            jax.ShapeDtypeStruct((1,), f32),
        ),
        in_specs=[anym] * 9,
        out_specs=(vmem, smem),
        scratch_shapes=[
            pltpu.SMEM((PAIRS, ALPHA * BLK), i32),
            pltpu.SMEM((BLK, PAIRS), i32),
            pltpu.VMEM((SLAB, BLK * ABLK), bf16),
            pltpu.VMEM((BLK, SLAB, ABLK), bf16),
            pltpu.VMEM((ALPHA, FETCH_CAP, SLAB, ABLK), bf16),
            pltpu.VMEM((NP, NP), f32),
            pltpu.VMEM((SLAB, NB), i32),
            pltpu.VMEM((SLAB, NB), f32),
            pltpu.VMEM((BLK, PAIRS, LINKS), i32),
            pltpu.VMEM((BLK, PAIRS, LINKS), i32),
            pltpu.VMEM((BLK, PAIRS, LINKS), f32),
            pltpu.VMEM((ALPHA * FETCH_CAP, SLAB, ABLK), bf16),
            pltpu.VMEM((2, SLAB, HALF), f32),
            pltpu.VMEM((NB, HALF), f32),
            pltpu.VMEM((4, BLK, SLAB, PAIRS * ABLK), bf16),
            pltpu.VMEM((NB * KROWS, HALF), f32),
            rows, rows, rows, rows, rows, rows,
            pltpu.VMEM((BLK, 128, 128), f32),
            pltpu.VMEM((BLK, 32, 128), f32),
            pltpu.VMEM((GROUPS * 4, BLK * CAP, HALF), bf16),
            pltpu.VMEM((BLK, GROUPS * 4 * CAP, NB), bf16),
            pltpu.VMEM((CHUNKS, 8, SLAB, SPAN * ABLK), f32),
            pltpu.VMEM((CHUNKS, 16, SLAB, SPAN * ABLK), bf16),
            pltpu.VMEM((16, 8, 128), f32),
            dma((9,)), dma((15,)), dma((15,)), dma((7,)), dma((7,)), dma((2,)), dma((2,)),
            dma((2, 2)), dma((2, 2)), dma((CHUNKS, 7)), dma((CHUNKS, 7)), dma((3,)), dma((3,)), dma((6,)), dma((6,)),
        ],
        compiler_params=pltpu.CompilerParams(
            vmem_limit_bytes=60 << 20, collective_id=0, has_side_effects=True
        ),
        name="sigma_links",
    )(amplitudes.T, integrals, beta_pair, beta_coef, pair_src.T, link_col, link_row, link_coef, link_count)
    out = lax.cond(
        most[0] >= CAP,
        lambda: by_links(amplitudes, integrals, beta_pair, beta_coef, pair_src, link_row, link_col, link_coef,
                         link_count).T,
        lambda: sigma,
    )
    return out.T


def solution(mesh):
    in_specs = (P("alpha", "beta"), P(), P("beta", None), P("beta", None), P(),
                P("alpha", None, None), P("alpha", None, None), P("alpha", None, None), P("alpha", None))
    return jax.shard_map(body, mesh=mesh, in_specs=in_specs, out_specs=P("alpha", "beta"), check_vma=False)
```

```python
import jax
import jax.numpy as jnp
from jax import lax
from jax.experimental import pallas as pl
from jax.experimental.pallas import tpu as pltpu
from jax.sharding import PartitionSpec as P

NP = 324
ABLK = 128
LINKS = 1024
PAIRS = 4
BLK = 4
NB = 256
SLAB = 32
ALPHA = 16
HALF = 128
QUART = 81
KROWS = 88
KHIP = 80
FETCH_CAP = 2
CAP = 32
GROUPS = 21
GCHUNK = 7
CHUNKS = 2
SPAN = BLK // CHUNKS
NTDIMS = (((1,), (1,)), ((), ()))
f32, bf16, i32 = jnp.float32, jnp.bfloat16, jnp.int32
MESH = pl.DeviceIdType.MESH


def dot(a, b):
    return jnp.dot(a, b, preferred_element_type=f32)


def dot_nt(a, b):
    return lax.dot_general(a, b, NTDIMS, preferred_element_type=f32)


def iota(shape, dim):
    return lax.broadcasted_iota(i32, shape, dim)


def hot_bf16(mask):
    return mask.astype(f32).astype(bf16)


def asked_range(src, device, first):
    low, high = jnp.int32(BLK - 1), jnp.int32(0)
    for t in range(BLK):
        for p in range(PAIRS):
            j = src[p, device * BLK + t] - first
            here = (j >> 2) == 0
            low = jnp.minimum(low, jnp.where(here, j, BLK - 1))
            high = jnp.maximum(high, jnp.where(here, j, 0))
    return low, high


def my_integrals(integ, first):
    rows = hot_bf16(iota((KROWS, NP), 1) - first == iota((KROWS, NP), 0))
    rows = jnp.where(iota((KROWS, NP), 0) < QUART, rows, jnp.zeros((), bf16))
    mine = dot(rows, integ[...].astype(bf16)).astype(bf16)
    shift = hot_bf16(iota((NP, 128), 0) - 256 == iota((NP, 128), 1))
    return mine[:, :256], dot(mine, shift).astype(bf16)[:, :KHIP]


def build_coupled(v_ref, ints, coup, begin, end):
    lo_ids = iota((256, 256), 0).astype(f32)
    hi_ids = iota((KHIP, 256), 0).astype(f32) + 256.0
    ints_lo, ints_hi = ints

    def one(i, carry):
        v = jnp.concatenate([v_ref[pl.ds(i * 2, 1), :], v_ref[pl.ds(i * 2 + 1, 1), :]], axis=1)
        where_to = jnp.abs(v) - 1.0
        sign = jnp.where(v < 0.0, -1.0, 1.0)
        hot_lo = jnp.where(lo_ids == where_to, sign, 0.0).astype(bf16)
        hot_hi = jnp.where(hi_ids == where_to, sign, 0.0).astype(bf16)
        out = dot(ints_lo, hot_lo) + dot(ints_hi, hot_hi)
        for h in range(2):
            start = pl.multiple_of((i * 2 + h) * KROWS, 8)
            coup[pl.ds(start, KROWS), :] = out[:, h * HALF : (h + 1) * HALF]
        return carry

    lax.fori_loop(begin // 2, end // 2, one, 0, unroll=32)


def rank_links(klq, rank):
    tri = hot_bf16(iota((256, 384), 0) <= iota((256, 384), 1))
    kl_ids = iota((KROWS, 256), 0).astype(f32)

    def one(p, carry):
        carry = list(carry)
        for c in range(4):
            hots = []
            for t in range(BLK):
                row = klq[pl.ds(t * PAIRS + p, 1), c * 256 : (c + 1) * 256]
                hots.append(kl_ids == row)
            stacked = jnp.concatenate([hot_bf16(h) for h in hots], axis=0)
            cum = dot(stacked, tri)
            for t in range(BLK):
                part = cum[t * KROWS : (t + 1) * KROWS]
                base = jnp.concatenate([carry[t], carry[t]], axis=1)
                mine = jnp.where(hots[t], part[:, :256] + base, 0.0)
                got = jnp.sum(mine, axis=0, keepdims=True) - 1.0
                rank[pl.ds(t * PAIRS + p, 1), c * 256 : (c + 1) * 256] = got
                carry[t] = carry[t] + part[:, 256:]
        return tuple(carry)

    zero = jnp.zeros((KROWS, 128), f32)
    lax.fori_loop(0, PAIRS, one, (zero,) * BLK, unroll=2)


def fill_tables(lo, hi, u1, u2, t1, t2):
    lo_ids = iota((128, LINKS), 0).astype(f32)
    hi_ids = iota((32, LINKS), 0).astype(f32)

    def target(t, carry):
        a1 = jnp.zeros((128, 32), f32)
        a2 = jnp.zeros((32, 128), f32)
        for p in range(PAIRS):
            i = t * PAIRS + p
            here = lo_ids == lo[pl.ds(i, 1), :]
            v1 = jnp.where(here, u1[pl.ds(i, 1), :], 0.0).astype(bf16)
            v2 = jnp.where(here, u2[pl.ds(i, 1), :], 0.0).astype(bf16)
            group = hot_bf16(hi_ids == hi[pl.ds(i, 1), :])
            a1 = a1 + dot_nt(v1, group)
            a2 = a2 + dot_nt(group, v2)
        t1[t] = jnp.concatenate([a1, jnp.zeros((128, 96), f32)], axis=1)
        t2[t] = a2
        return carry

    lax.fori_loop(0, BLK, target, 0, unroll=2)


def gather_rows(at, t1, gs, t):
    tables = [((128 + iota((128, 128), 1)) * (1 << p)).astype(f32) for p in range(2)]
    amps = at[:, t].reshape(HALF, PAIRS * ABLK)
    amps = jnp.concatenate([amps[:, : 2 * ABLK], amps[:, 2 * ABLK :]], axis=0)
    for c in range(GROUPS // GCHUNK):
        hots, later = [], []
        for h in range(GCHUNK):
            code = jnp.take_along_axis(t1[t], jnp.full((128, 128), c * GCHUNK + h, i32), axis=1)
            size = jnp.abs(code)
            sign = jnp.where(code < 0.0, -1.0, 1.0)
            later.append(size >= 512.0)
            size = jnp.where(later[h], size * 0.25, size)
            hots.append(
                jnp.concatenate([jnp.where(size == tab, sign, 0.0).astype(bf16) for tab in tables], axis=1)
            )
        both = dot_nt(jnp.concatenate(hots, axis=0), amps)
        for h in range(GCHUNK):
            two = both[h * 128 : (h + 1) * 128]
            rows = jnp.where(later[h], two[:, HALF:], two[:, :HALF]).astype(bf16)
            for k in range(4):
                gs[(c * GCHUNK + h) * 4 + k, t * CAP : (t + 1) * CAP, :] = rows[k * CAP : (k + 1) * CAP]


def pick(coup, gs, ps):
    def one(kl, carry):
        c = coup[pl.ds(kl, NB, stride=KROWS), :].astype(bf16)
        q = dot_nt(gs[kl], c).astype(bf16)
        start = pl.multiple_of(kl * CAP, CAP)
        for t in range(BLK):
            ps[t, pl.ds(start, CAP), :] = q[t * CAP : (t + 1) * CAP]
        return carry

    lax.fori_loop(0, QUART, one, 0, unroll=27)
    for t in range(BLK):
        ps[t, QUART * CAP :, :] = jnp.zeros((4 * CAP * GROUPS - QUART * CAP, NB), bf16)


def add_rows(t2, ps, t):
    ids = iota((128, 128), 0).astype(f32)
    hot = jnp.concatenate([hot_bf16(ids == t2[t, g : g + 1, :]) for g in range(GROUPS)], axis=1)
    return dot(hot, ps[t])


def kernel(amp_h, integ_h, pair_h, coef_h, src_h, col_h, row_h, lcoef_h, count_h, out, flag_out,
           src, count, amp, blocks, give, integ, pair, coef, col, row, lcoef, ev, vown, vall, at, coup, klq, rank, lo, hi, u1, u2,
           t1, t2, gs, ps, sb, rb, fl, in_sem, a_send, a_recv, v_send, v_recv, y_send, y_recv, s_send,
           s_recv, r_send, r_recv, f_send, f_recv, g_send, g_recv):
    a, b = lax.axis_index("alpha"), lax.axis_index("beta")
    core = b % 2
    half, q = b // 4, b % 4
    x, z = a // 4, a % 4
    sibling = b // 2 * 2 + 1 - core
    across = half * 4 + (q + 2) % 4
    peers = [(b + k) % 8 for k in range(1, 8)]
    mates = [half * 4 + (q + k) % 4 for k in range(1, 4)]

    offsets = sorted(
        ((dx, dz) for dx in range(4) for dz in range(4)),
        key=lambda d: (-min(d[0], 4 - d[0]) - min(d[1], 4 - d[1]), d),
    )

    loads = []
    for n, (h, m) in enumerate([(amp_h, amp), (pair_h, pair), (coef_h, coef), (col_h, col), (row_h, row),
                                (lcoef_h, lcoef), (integ_h, integ), (src_h, src),
                                (count_h, count)]):
        loads.append(pltpu.make_async_copy(h, m, in_sem.at[n]))
        loads[-1].start()

    barrier = pltpu.get_barrier_semaphore()
    for k in range(1, ALPHA):
        pl.semaphore_signal(barrier, inc=1, device_id=((a + k) % ALPHA, b), device_id_type=MESH)
    for k in range(1, 8):
        pl.semaphore_signal(barrier, inc=1, device_id=(a, (b + k) % 8), device_id_type=MESH)

    loads[0].wait()
    loads[7].wait()
    for j in range(BLK):
        blocks[j] = amp[:, j * ABLK : (j + 1) * ABLK]
    for k, (dx, dz) in enumerate(offsets):
        to = (x + dx) % 4 * 4 + (z + dz) % 4
        for n, j in enumerate(asked_range(src, to, a * BLK)):
            give[k, n] = blocks[j]
    ev[pl.ds(a * FETCH_CAP, FETCH_CAP)] = give[ALPHA - 1]
    loads[1].wait()
    loads[2].wait()
    mine = pl.ds(pl.multiple_of(b * SLAB, SLAB), SLAB)
    codes = coef[...] * (pair[...] + 1).astype(f32)
    for h in range(2):
        vown[h] = codes[:, h * HALF : (h + 1) * HALF]
    vall[mine, :] = vown[half]
    pl.semaphore_wait(barrier, ALPHA - 1 + 7)

    def remote(source, target, send, recv, to):
        c = pltpu.make_async_remote_copy(src_ref=source, dst_ref=target, send_sem=send, recv_sem=recv,
                                         device_id=to, device_id_type=MESH)
        c.start()
        return c

    a_copies = [
        remote(give.at[k], ev.at[pl.ds(a * FETCH_CAP, FETCH_CAP)], a_send.at[k], a_recv.at[k],
               ((x + dx) % 4 * 4 + (z + dz) % 4, b))
        for k, (dx, dz) in enumerate(offsets[:-1])
    ]
    v_copies = [
        remote(vown.at[m // 4], vall.at[mine], v_send.at[k], v_recv.at[k], (a, m)) for k, m in enumerate(peers)
    ]

    asked = [src[p, a * BLK + t] for t in range(BLK) for p in range(PAIRS)]
    owners = [block >> 2 for block in asked]
    places = []
    for block, owner in zip(asked, owners):
        low = block
        for other, its in zip(asked, owners):
            low = jnp.minimum(low, jnp.where(its == owner, other, block))
        places.append(owner * FETCH_CAP + jnp.where(low == block, 0, 1))

    for n in (3, 4, 5, 8):
        loads[n].wait()
    for t in range(BLK):
        column = col[t]
        kl = (column >> 7) - q * QUART
        slot = iota((PAIRS, LINKS), 1)
        part = iota((PAIRS, LINKS), 0)
        full = jnp.zeros((PAIRS, LINKS), i32)
        for p in range(PAIRS):
            full = jnp.where(part == p, count[t, p], full)
        kl = jnp.where((slot < full) & (kl >= 0) & (kl < QUART), kl, -1)
        at_rows = slice(t * PAIRS, (t + 1) * PAIRS)
        klq[at_rows, :] = kl.astype(f32)
        u1[at_rows, :] = lcoef[t] * ((128 + (column & 127)) << part).astype(f32)
        u2[at_rows, :] = row[t].astype(f32)
    rank_links(klq, rank)
    kl = klq[...].astype(i32)
    r = rank[...].astype(i32)
    ok = (kl >= 0) & (r < CAP)
    lo[...] = jnp.where(ok, (kl & 3) * CAP + r, -1).astype(f32)
    hi[...] = jnp.where(ok, kl >> 2, -1).astype(f32)
    fl[q] = jnp.broadcast_to(jnp.max(rank[...], keepdims=True), (8, 128))
    f_copies = [
        remote(fl.at[q], fl.at[q], f_send.at[k], f_recv.at[k], (a, m)) for k, m in enumerate(mates)
    ]
    fill_tables(lo, hi, u1, u2, t1, t2)

    loads[6].wait()
    ints = my_integrals(integ, q * QUART)
    for c in a_copies:
        c.wait_recv()
    y_copies, s_copies = [], []
    for t in range(BLK):
        for p in range(PAIRS):
            at[q, t, :, p * ABLK : (p + 1) * ABLK] = ev[places[t * PAIRS + p]]
        if t % 2:
            pair = pl.ds(t - 1, 2)
            mine, n = at.at[q, pair], t // 2
            y_copies.append(remote(mine, mine, y_send.at[n], y_recv.at[n], (a, across)))
            s_copies.append([remote(mine, mine, s_send.at[n, 0], s_recv.at[n, 0], (a, sibling))])

    for c in v_copies:
        c.wait_recv()
    for c in f_copies:
        c.wait_recv()
    fl[8] = jnp.maximum(jnp.maximum(fl[0], fl[1]), jnp.maximum(fl[2], fl[3]))
    g_copies = [
        remote(fl.at[8], fl.at[8 + k], g_send.at[k - 1], g_recv.at[k - 1], (x * 4 + (z + k) % 4, b))
        for k in range(1, 4)
    ]
    for t in range(BLK):
        build_coupled(vall, ints, coup, t * 64, t * 64 + 64)
        if t in (1, 2):
            y_copies[t - 1].wait_recv()
            away = at.at[(q + 2) % 4, pl.ds(t * 2 - 2, 2)]
            s_copies[t - 1].append(
                remote(away, away, s_send.at[t - 1, 1], s_recv.at[t - 1, 1], (a, sibling))
            )
    for c in g_copies:
        c.wait_recv()
    fl[12] = jnp.maximum(jnp.maximum(fl[8], fl[9]), jnp.maximum(fl[10], fl[11]))
    g_copies += [
        remote(fl.at[12], fl.at[12 + k], g_send.at[2 + k], g_recv.at[2 + k], ((x + k) % 4 * 4 + z, b))
        for k in range(1, 4)
    ]
    for t in range(BLK):
        if t % 2 == 0:
            for c in s_copies[t // 2]:
                c.wait_recv()
        gather_rows(at, t1, gs, t)
    pick(coup, gs, ps)
    r_copies = []
    for n in range(CHUNKS):
        parts = [add_rows(t2, ps, n * SPAN + i).T for i in range(SPAN)]
        for k in range(8):
            slab = jnp.concatenate([part[k * SLAB : (k + 1) * SLAB] for part in parts], axis=1)
            sb[n, k] = slab
            rb[n, 8 + k] = slab.astype(bf16)
        r_copies.append([
            remote(rb.at[n, 8 + peers[k]], rb.at[n, b], r_send.at[n, k], r_recv.at[n, k], (a, peers[k]))
            for k in (3, 2, 4, 1, 5, 0, 6)
        ])
    for c in a_copies + v_copies + f_copies + g_copies + y_copies + sum(s_copies, []):
        c.wait_send()
    for n in range(CHUNKS):
        for c in r_copies[n]:
            c.wait_recv()
        total = sb[n, b]
        for k in range(1, 8):
            total = total + rb[n, (b + 8 - k) % 8].astype(f32)
        out[:, n * SPAN * ABLK : (n + 1) * SPAN * ABLK] = total
    for c in g_copies[3:]:
        c.wait_recv()
    flag_out[0] = jnp.max(fl[12:16])
    for c in sum(r_copies, []):
        c.wait_send()


def assemble(local_amp, pair_src, num_local):
    alpha_count = lax.axis_size("alpha")
    my_index = lax.axis_index("alpha")
    block_total = pair_src.shape[0]
    block_rows = local_amp.shape[1]
    slab_width = local_amp.shape[2]
    my_requests = lax.dynamic_slice_in_dim(pair_src, my_index * num_local, num_local, 0)
    owned_ids = my_index * num_local + jnp.arange(num_local, dtype=jnp.int32)
    requests = pair_src.reshape(alpha_count, -1)
    asked_for = jnp.any(requests[:, :, None] == owned_ids[None, None, :], axis=1)
    position = jnp.cumsum(asked_for.astype(jnp.int32), axis=1) - 1
    slot_ids = jnp.arange(FETCH_CAP, dtype=jnp.int32)
    select = (asked_for[:, None, :] & (position[:, None, :] == slot_ids[None, :, None])).astype(
        local_amp.dtype
    )
    outgoing = jnp.einsum(
        "qsj,jab->qsab", select, local_amp, preferred_element_type=jnp.float32
    ).astype(local_amp.dtype)
    incoming = lax.all_to_all(outgoing, "alpha", split_axis=0, concat_axis=0, tiled=True)
    combined = jnp.concatenate([local_amp, incoming.reshape(-1, block_rows, slab_width)], axis=0)
    catalog = jnp.arange(block_total, dtype=jnp.int32).reshape(alpha_count, num_local)
    wanted = jnp.any(my_requests.reshape(-1)[:, None, None] == catalog[None], axis=0)
    order_pos = jnp.cumsum(wanted.astype(jnp.int32), axis=1) - 1
    owner_dev = my_requests // num_local
    within = my_requests % num_local
    remote = num_local + owner_dev * FETCH_CAP + order_pos[owner_dev, within]
    return (combined, jnp.where(owner_dev == my_index, within, remote))


def by_links(
    amplitudes, integrals, beta_pair, beta_coef, pair_src, link_row, link_col, link_coef, link_count
):
    num_local = link_row.shape[0]
    slab_piece = amplitudes.shape[1]
    local_amp = amplitudes.reshape(num_local, ABLK, slab_piece)
    full_rows = lax.all_gather(local_amp, "beta", axis=2, tiled=True)
    gathered, sources = assemble(full_rows, pair_src, num_local)
    pair_ids = jnp.arange(NP, dtype=jnp.int32)
    pair_hot = (beta_pair[None, :, :] == pair_ids[:, None, None]).astype(jnp.float32)
    looked_up = jnp.einsum("ki,ibj->kbj", integrals, pair_hot, precision=lax.Precision.HIGHEST)
    coupled = (looked_up * beta_coef[None]).astype(jnp.bfloat16)
    link_ids = jnp.arange(LINKS, dtype=jnp.int32)
    string_ids = jnp.arange(ABLK, dtype=jnp.int32)

    def per_target(target, sigma_acc):
        chosen = lax.dynamic_index_in_dim(sources, target, 0, keepdims=False)
        columns = lax.dynamic_index_in_dim(link_col, target, 0, keepdims=False)
        occupied = lax.dynamic_index_in_dim(link_count, target, 0, keepdims=False)
        signs = lax.dynamic_index_in_dim(link_coef, target, 0, keepdims=False)
        targets_row = lax.dynamic_index_in_dim(link_row, target, 0, keepdims=False)

        def per_pair(total, pair_index):
            block = jnp.take(gathered, chosen[pair_index], axis=0)
            column_row = columns[pair_index]
            orbital_pair = column_row // ABLK
            source_row = column_row % ABLK
            amp_rows = jnp.take(block, source_row, axis=0)
            coupled_rows = jnp.take(coupled, orbital_pair, axis=0)
            picked = jnp.einsum(
                "lbj,lj->lb", coupled_rows, amp_rows, preferred_element_type=jnp.float32
            )
            weights = jnp.where(
                link_ids < occupied[pair_index], signs[pair_index], jnp.float32(0.0)
            )
            hot_rows = (targets_row[pair_index][:, None] == string_ids[None, :]).astype(jnp.float32)
            added = jnp.dot(
                hot_rows.T,
                picked * weights[:, None],
                precision=lax.Precision.HIGHEST,
                preferred_element_type=jnp.float32,
            )
            return (total + added, None)

        start = jnp.zeros((ABLK, slab_piece), jnp.float32)
        result, unused = lax.scan(per_pair, start, jnp.arange(chosen.shape[0], dtype=jnp.int32))
        return lax.dynamic_update_index_in_dim(sigma_acc, result, target, 0)

    sigma_acc = jnp.zeros((num_local, ABLK, slab_piece), jnp.float32)
    sigma_acc = lax.fori_loop(0, num_local, per_target, sigma_acc)
    return sigma_acc.reshape(num_local * ABLK, slab_piece)


def body(amplitudes, integrals, beta_pair, beta_coef, pair_src, link_row, link_col, link_coef, link_count):
    anym = pl.BlockSpec(memory_space=pl.ANY)
    smem = pl.BlockSpec(memory_space=pltpu.SMEM)
    vmem = pl.BlockSpec(memory_space=pltpu.VMEM)
    rows = pltpu.VMEM((BLK * PAIRS, LINKS), f32)
    dma = pltpu.SemaphoreType.DMA
    sigma, most = pl.pallas_call(
        kernel,
        out_shape=(
            jax.ShapeDtypeStruct((SLAB, BLK * ABLK), f32),
            jax.ShapeDtypeStruct((1,), f32),
        ),
        in_specs=[anym] * 9,
        out_specs=(vmem, smem),
        scratch_shapes=[
            pltpu.SMEM((PAIRS, ALPHA * BLK), i32),
            pltpu.SMEM((BLK, PAIRS), i32),
            pltpu.VMEM((SLAB, BLK * ABLK), bf16),
            pltpu.VMEM((BLK, SLAB, ABLK), bf16),
            pltpu.VMEM((ALPHA, FETCH_CAP, SLAB, ABLK), bf16),
            pltpu.VMEM((NP, NP), f32),
            pltpu.VMEM((SLAB, NB), i32),
            pltpu.VMEM((SLAB, NB), f32),
            pltpu.VMEM((BLK, PAIRS, LINKS), i32),
            pltpu.VMEM((BLK, PAIRS, LINKS), i32),
            pltpu.VMEM((BLK, PAIRS, LINKS), f32),
            pltpu.VMEM((ALPHA * FETCH_CAP, SLAB, ABLK), bf16),
            pltpu.VMEM((2, SLAB, HALF), f32),
            pltpu.VMEM((NB, HALF), f32),
            pltpu.VMEM((4, BLK, SLAB, PAIRS * ABLK), bf16),
            pltpu.VMEM((NB * KROWS, HALF), f32),
            rows, rows, rows, rows, rows, rows,
            pltpu.VMEM((BLK, 128, 128), f32),
            pltpu.VMEM((BLK, 32, 128), f32),
            pltpu.VMEM((GROUPS * 4, BLK * CAP, HALF), bf16),
            pltpu.VMEM((BLK, GROUPS * 4 * CAP, NB), bf16),
            pltpu.VMEM((CHUNKS, 8, SLAB, SPAN * ABLK), f32),
            pltpu.VMEM((CHUNKS, 16, SLAB, SPAN * ABLK), bf16),
            pltpu.VMEM((16, 8, 128), f32),
            dma((9,)), dma((15,)), dma((15,)), dma((7,)), dma((7,)), dma((2,)), dma((2,)),
            dma((2, 2)), dma((2, 2)), dma((CHUNKS, 7)), dma((CHUNKS, 7)), dma((3,)), dma((3,)), dma((6,)), dma((6,)),
        ],
        compiler_params=pltpu.CompilerParams(
            vmem_limit_bytes=60 << 20, collective_id=0, has_side_effects=True
        ),
        name="sigma_links",
    )(amplitudes.T, integrals, beta_pair, beta_coef, pair_src.T, link_col, link_row, link_coef, link_count)
    out = lax.cond(
        most[0] >= CAP,
        lambda: by_links(amplitudes, integrals, beta_pair, beta_coef, pair_src, link_row, link_col, link_coef,
                         link_count).T,
        lambda: sigma,
    )
    return out.T


def solution(mesh):
    in_specs = (P("alpha", "beta"), P(), P("beta", None), P("beta", None), P(),
                P("alpha", None, None), P("alpha", None, None), P("alpha", None, None), P("alpha", None))
    return jax.shard_map(body, mesh=mesh, in_specs=in_specs, out_specs=P("alpha", "beta"), check_vma=False)
```

```python
import jax
import jax.numpy as jnp
from jax import lax
from jax.experimental import pallas as pl
from jax.experimental.pallas import tpu as pltpu
from jax.sharding import PartitionSpec as P

NP = 324
ABLK = 128
LINKS = 1024
PAIRS = 4
BLK = 4
NB = 256
SLAB = 32
ALPHA = 16
HALF = 128
QUART = 81
KROWS = 88
KHIP = 80
FETCH_CAP = 2
CAP = 32
GROUPS = 21
GCHUNK = 7
CHUNKS = 2
SPAN = BLK // CHUNKS
NTDIMS = (((1,), (1,)), ((), ()))
f32, bf16, i32 = jnp.float32, jnp.bfloat16, jnp.int32
MESH = pl.DeviceIdType.MESH


def dot(a, b):
    return jnp.dot(a, b, preferred_element_type=f32)


def dot_nt(a, b):
    return lax.dot_general(a, b, NTDIMS, preferred_element_type=f32)


def iota(shape, dim):
    return lax.broadcasted_iota(i32, shape, dim)


def hot_bf16(mask):
    return mask.astype(f32).astype(bf16)


def asked_range(src, device, first):
    low, high = jnp.int32(BLK - 1), jnp.int32(0)
    for t in range(BLK):
        for p in range(PAIRS):
            j = src[p, device * BLK + t] - first
            here = (j >> 2) == 0
            low = jnp.minimum(low, jnp.where(here, j, BLK - 1))
            high = jnp.maximum(high, jnp.where(here, j, 0))
    return low, high


def my_integrals(integ, first):
    rows = hot_bf16(iota((KROWS, NP), 1) - first == iota((KROWS, NP), 0))
    rows = jnp.where(iota((KROWS, NP), 0) < QUART, rows, jnp.zeros((), bf16))
    mine = dot(rows, integ[...].astype(bf16)).astype(bf16)
    shift = hot_bf16(iota((NP, 128), 0) - 256 == iota((NP, 128), 1))
    return mine[:, :256], dot(mine, shift).astype(bf16)[:, :KHIP]


def build_coupled(v_ref, ints, coup, begin, end):
    lo_ids = iota((256, 256), 0).astype(f32)
    hi_ids = iota((KHIP, 256), 0).astype(f32) + 256.0
    ints_lo, ints_hi = ints

    def one(i, carry):
        v = jnp.concatenate([v_ref[pl.ds(i * 2, 1), :], v_ref[pl.ds(i * 2 + 1, 1), :]], axis=1)
        where_to = jnp.abs(v) - 1.0
        sign = jnp.where(v < 0.0, -1.0, 1.0)
        hot_lo = jnp.where(lo_ids == where_to, sign, 0.0).astype(bf16)
        hot_hi = jnp.where(hi_ids == where_to, sign, 0.0).astype(bf16)
        out = dot(ints_lo, hot_lo) + dot(ints_hi, hot_hi)
        for h in range(2):
            start = pl.multiple_of((i * 2 + h) * KROWS, 8)
            coup[pl.ds(start, KROWS), :] = out[:, h * HALF : (h + 1) * HALF]
        return carry

    lax.fori_loop(begin // 2, end // 2, one, 0, unroll=32)


def rank_links(klq, rank):
    tri = hot_bf16(iota((256, 384), 0) <= iota((256, 384), 1))
    kl_ids = iota((KROWS, 256), 0).astype(f32)

    def one(p, carry):
        carry = list(carry)
        for c in range(4):
            hots = []
            for t in range(BLK):
                row = klq[pl.ds(t * PAIRS + p, 1), c * 256 : (c + 1) * 256]
                hots.append(kl_ids == row)
            stacked = jnp.concatenate([hot_bf16(h) for h in hots], axis=0)
            cum = dot(stacked, tri)
            for t in range(BLK):
                part = cum[t * KROWS : (t + 1) * KROWS]
                base = jnp.concatenate([carry[t], carry[t]], axis=1)
                mine = jnp.where(hots[t], part[:, :256] + base, 0.0)
                got = jnp.sum(mine, axis=0, keepdims=True) - 1.0
                rank[pl.ds(t * PAIRS + p, 1), c * 256 : (c + 1) * 256] = got
                carry[t] = carry[t] + part[:, 256:]
        return tuple(carry)

    zero = jnp.zeros((KROWS, 128), f32)
    lax.fori_loop(0, PAIRS, one, (zero,) * BLK, unroll=4)


def fill_tables(lo, hi, u1, u2, t1, t2):
    lo_ids = iota((128, LINKS), 0).astype(f32)
    hi_ids = iota((32, LINKS), 0).astype(f32)

    def target(t, carry):
        a1 = jnp.zeros((128, 32), f32)
        a2 = jnp.zeros((32, 128), f32)
        for p in range(PAIRS):
            i = t * PAIRS + p
            here = lo_ids == lo[pl.ds(i, 1), :]
            v1 = jnp.where(here, u1[pl.ds(i, 1), :], 0.0).astype(bf16)
            v2 = jnp.where(here, u2[pl.ds(i, 1), :], 0.0).astype(bf16)
            group = hot_bf16(hi_ids == hi[pl.ds(i, 1), :])
            a1 = a1 + dot_nt(v1, group)
            a2 = a2 + dot_nt(group, v2)
        t1[t] = jnp.concatenate([a1, jnp.zeros((128, 96), f32)], axis=1)
        t2[t] = a2
        return carry

    lax.fori_loop(0, BLK, target, 0, unroll=4)


def gather_rows(at, t1, gs, t):
    tables = [((128 + iota((128, 128), 1)) * (1 << p)).astype(f32) for p in range(2)]
    amps = at[:, t].reshape(HALF, PAIRS * ABLK)
    amps = jnp.concatenate([amps[:, : 2 * ABLK], amps[:, 2 * ABLK :]], axis=0)
    for c in range(GROUPS // GCHUNK):
        hots, later = [], []
        for h in range(GCHUNK):
            code = jnp.take_along_axis(t1[t], jnp.full((128, 128), c * GCHUNK + h, i32), axis=1)
            size = jnp.abs(code)
            sign = jnp.where(code < 0.0, -1.0, 1.0)
            later.append(size >= 512.0)
            size = jnp.where(later[h], size * 0.25, size)
            hots.append(
                jnp.concatenate([jnp.where(size == tab, sign, 0.0).astype(bf16) for tab in tables], axis=1)
            )
        both = dot_nt(jnp.concatenate(hots, axis=0), amps)
        for h in range(GCHUNK):
            two = both[h * 128 : (h + 1) * 128]
            rows = jnp.where(later[h], two[:, HALF:], two[:, :HALF]).astype(bf16)
            for k in range(4):
                gs[(c * GCHUNK + h) * 4 + k, t * CAP : (t + 1) * CAP, :] = rows[k * CAP : (k + 1) * CAP]


def pick(coup, gs, ps):
    def one(kl, carry):
        c = coup[pl.ds(kl, NB, stride=KROWS), :].astype(bf16)
        q = dot_nt(gs[kl], c).astype(bf16)
        start = pl.multiple_of(kl * CAP, CAP)
        for t in range(BLK):
            ps[t, pl.ds(start, CAP), :] = q[t * CAP : (t + 1) * CAP]
        return carry

    lax.fori_loop(0, QUART, one, 0, unroll=27)
    for t in range(BLK):
        ps[t, QUART * CAP :, :] = jnp.zeros((4 * CAP * GROUPS - QUART * CAP, NB), bf16)


def add_rows(t2, ps, t):
    ids = iota((128, 128), 0).astype(f32)
    hot = jnp.concatenate([hot_bf16(ids == t2[t, g : g + 1, :]) for g in range(GROUPS)], axis=1)
    return dot(hot, ps[t])


def kernel(amp_h, integ_h, pair_h, coef_h, src_h, col_h, row_h, lcoef_h, count_h, out, flag_out,
           src, count, amp, blocks, give, integ, pair, coef, col, row, lcoef, ev, vown, vall, at, coup, klq, rank, lo, hi, u1, u2,
           t1, t2, gs, ps, sb, rb, fl, in_sem, a_send, a_recv, v_send, v_recv, y_send, y_recv, s_send,
           s_recv, r_send, r_recv, f_send, f_recv, g_send, g_recv):
    a, b = lax.axis_index("alpha"), lax.axis_index("beta")
    core = b % 2
    half, q = b // 4, b % 4
    x, z = a // 4, a % 4
    sibling = b // 2 * 2 + 1 - core
    across = half * 4 + (q + 2) % 4
    peers = [(b + k) % 8 for k in range(1, 8)]
    mates = [half * 4 + (q + k) % 4 for k in range(1, 4)]

    offsets = sorted(
        ((dx, dz) for dx in range(4) for dz in range(4)),
        key=lambda d: (-min(d[0], 4 - d[0]) - min(d[1], 4 - d[1]), d),
    )

    loads = []
    for n, (h, m) in enumerate([(amp_h, amp), (pair_h, pair), (coef_h, coef), (col_h, col), (row_h, row),
                                (lcoef_h, lcoef), (integ_h, integ), (src_h, src),
                                (count_h, count)]):
        loads.append(pltpu.make_async_copy(h, m, in_sem.at[n]))
        loads[-1].start()

    barrier = pltpu.get_barrier_semaphore()
    for k in range(1, ALPHA):
        pl.semaphore_signal(barrier, inc=1, device_id=((a + k) % ALPHA, b), device_id_type=MESH)
    for k in range(1, 8):
        pl.semaphore_signal(barrier, inc=1, device_id=(a, (b + k) % 8), device_id_type=MESH)

    loads[0].wait()
    loads[7].wait()
    for j in range(BLK):
        blocks[j] = amp[:, j * ABLK : (j + 1) * ABLK]
    for k, (dx, dz) in enumerate(offsets):
        to = (x + dx) % 4 * 4 + (z + dz) % 4
        for n, j in enumerate(asked_range(src, to, a * BLK)):
            give[k, n] = blocks[j]
    ev[pl.ds(a * FETCH_CAP, FETCH_CAP)] = give[ALPHA - 1]
    loads[1].wait()
    loads[2].wait()
    mine = pl.ds(pl.multiple_of(b * SLAB, SLAB), SLAB)
    codes = coef[...] * (pair[...] + 1).astype(f32)
    for h in range(2):
        vown[h] = codes[:, h * HALF : (h + 1) * HALF]
    vall[mine, :] = vown[half]
    pl.semaphore_wait(barrier, ALPHA - 1 + 7)

    def remote(source, target, send, recv, to):
        c = pltpu.make_async_remote_copy(src_ref=source, dst_ref=target, send_sem=send, recv_sem=recv,
                                         device_id=to, device_id_type=MESH)
        c.start()
        return c

    a_copies = [
        remote(give.at[k], ev.at[pl.ds(a * FETCH_CAP, FETCH_CAP)], a_send.at[k], a_recv.at[k],
               ((x + dx) % 4 * 4 + (z + dz) % 4, b))
        for k, (dx, dz) in enumerate(offsets[:-1])
    ]
    v_copies = [
        remote(vown.at[m // 4], vall.at[mine], v_send.at[k], v_recv.at[k], (a, m)) for k, m in enumerate(peers)
    ]

    asked = [src[p, a * BLK + t] for t in range(BLK) for p in range(PAIRS)]
    owners = [block >> 2 for block in asked]
    places = []
    for block, owner in zip(asked, owners):
        low = block
        for other, its in zip(asked, owners):
            low = jnp.minimum(low, jnp.where(its == owner, other, block))
        places.append(owner * FETCH_CAP + jnp.where(low == block, 0, 1))

    for n in (3, 4, 5, 8):
        loads[n].wait()
    for t in range(BLK):
        column = col[t]
        kl = (column >> 7) - q * QUART
        slot = iota((PAIRS, LINKS), 1)
        part = iota((PAIRS, LINKS), 0)
        full = jnp.zeros((PAIRS, LINKS), i32)
        for p in range(PAIRS):
            full = jnp.where(part == p, count[t, p], full)
        kl = jnp.where((slot < full) & (kl >= 0) & (kl < QUART), kl, -1)
        at_rows = slice(t * PAIRS, (t + 1) * PAIRS)
        klq[at_rows, :] = kl.astype(f32)
        u1[at_rows, :] = lcoef[t] * ((128 + (column & 127)) << part).astype(f32)
        u2[at_rows, :] = row[t].astype(f32)
    rank_links(klq, rank)
    kl = klq[...].astype(i32)
    r = rank[...].astype(i32)
    ok = (kl >= 0) & (r < CAP)
    lo[...] = jnp.where(ok, (kl & 3) * CAP + r, -1).astype(f32)
    hi[...] = jnp.where(ok, kl >> 2, -1).astype(f32)
    fl[q] = jnp.broadcast_to(jnp.max(rank[...], keepdims=True), (8, 128))
    f_copies = [
        remote(fl.at[q], fl.at[q], f_send.at[k], f_recv.at[k], (a, m)) for k, m in enumerate(mates)
    ]
    fill_tables(lo, hi, u1, u2, t1, t2)

    loads[6].wait()
    ints = my_integrals(integ, q * QUART)
    for c in a_copies:
        c.wait_recv()
    y_copies, s_copies = [], []
    for t in range(BLK):
        for p in range(PAIRS):
            at[q, t, :, p * ABLK : (p + 1) * ABLK] = ev[places[t * PAIRS + p]]
        if t % 2:
            pair = pl.ds(t - 1, 2)
            mine, n = at.at[q, pair], t // 2
            y_copies.append(remote(mine, mine, y_send.at[n], y_recv.at[n], (a, across)))
            s_copies.append([remote(mine, mine, s_send.at[n, 0], s_recv.at[n, 0], (a, sibling))])

    for c in v_copies:
        c.wait_recv()
    for c in f_copies:
        c.wait_recv()
    fl[8] = jnp.maximum(jnp.maximum(fl[0], fl[1]), jnp.maximum(fl[2], fl[3]))
    g_copies = [
        remote(fl.at[8], fl.at[8 + k], g_send.at[k - 1], g_recv.at[k - 1], (x * 4 + (z + k) % 4, b))
        for k in range(1, 4)
    ]
    for t in range(BLK):
        build_coupled(vall, ints, coup, t * 64, t * 64 + 64)
        if t in (2, 3):
            y_copies[t - 2].wait_recv()
            away = at.at[(q + 2) % 4, pl.ds(t * 2 - 4, 2)]
            s_copies[t - 2].append(
                remote(away, away, s_send.at[t - 2, 1], s_recv.at[t - 2, 1], (a, sibling))
            )
    for c in g_copies:
        c.wait_recv()
    fl[12] = jnp.maximum(jnp.maximum(fl[8], fl[9]), jnp.maximum(fl[10], fl[11]))
    g_copies += [
        remote(fl.at[12], fl.at[12 + k], g_send.at[2 + k], g_recv.at[2 + k], ((x + k) % 4 * 4 + z, b))
        for k in range(1, 4)
    ]
    for t in range(BLK):
        if t % 2 == 0:
            for c in s_copies[t // 2]:
                c.wait_recv()
        gather_rows(at, t1, gs, t)
    pick(coup, gs, ps)
    r_copies = []
    for n in range(CHUNKS):
        parts = [add_rows(t2, ps, n * SPAN + i).T for i in range(SPAN)]
        for k in range(8):
            slab = jnp.concatenate([part[k * SLAB : (k + 1) * SLAB] for part in parts], axis=1)
            sb[n, k] = slab
            rb[n, 8 + k] = slab.astype(bf16)
        r_copies.append([
            remote(rb.at[n, 8 + peers[k]], rb.at[n, b], r_send.at[n, k], r_recv.at[n, k], (a, peers[k]))
            for k in (3, 2, 4, 1, 5, 0, 6)
        ])
    for c in a_copies + v_copies + f_copies + g_copies + y_copies + sum(s_copies, []):
        c.wait_send()
    for n in range(CHUNKS):
        for c in r_copies[n]:
            c.wait_recv()
        total = sb[n, b]
        for k in range(1, 8):
            total = total + rb[n, (b + 8 - k) % 8].astype(f32)
        out[:, n * SPAN * ABLK : (n + 1) * SPAN * ABLK] = total
    for c in g_copies[3:]:
        c.wait_recv()
    flag_out[0] = jnp.max(fl[12:16])
    for c in sum(r_copies, []):
        c.wait_send()


def assemble(local_amp, pair_src, num_local):
    alpha_count = lax.axis_size("alpha")
    my_index = lax.axis_index("alpha")
    block_total = pair_src.shape[0]
    block_rows = local_amp.shape[1]
    slab_width = local_amp.shape[2]
    my_requests = lax.dynamic_slice_in_dim(pair_src, my_index * num_local, num_local, 0)
    owned_ids = my_index * num_local + jnp.arange(num_local, dtype=jnp.int32)
    requests = pair_src.reshape(alpha_count, -1)
    asked_for = jnp.any(requests[:, :, None] == owned_ids[None, None, :], axis=1)
    position = jnp.cumsum(asked_for.astype(jnp.int32), axis=1) - 1
    slot_ids = jnp.arange(FETCH_CAP, dtype=jnp.int32)
    select = (asked_for[:, None, :] & (position[:, None, :] == slot_ids[None, :, None])).astype(
        local_amp.dtype
    )
    outgoing = jnp.einsum(
        "qsj,jab->qsab", select, local_amp, preferred_element_type=jnp.float32
    ).astype(local_amp.dtype)
    incoming = lax.all_to_all(outgoing, "alpha", split_axis=0, concat_axis=0, tiled=True)
    combined = jnp.concatenate([local_amp, incoming.reshape(-1, block_rows, slab_width)], axis=0)
    catalog = jnp.arange(block_total, dtype=jnp.int32).reshape(alpha_count, num_local)
    wanted = jnp.any(my_requests.reshape(-1)[:, None, None] == catalog[None], axis=0)
    order_pos = jnp.cumsum(wanted.astype(jnp.int32), axis=1) - 1
    owner_dev = my_requests // num_local
    within = my_requests % num_local
    remote = num_local + owner_dev * FETCH_CAP + order_pos[owner_dev, within]
    return (combined, jnp.where(owner_dev == my_index, within, remote))


def by_links(
    amplitudes, integrals, beta_pair, beta_coef, pair_src, link_row, link_col, link_coef, link_count
):
    num_local = link_row.shape[0]
    slab_piece = amplitudes.shape[1]
    local_amp = amplitudes.reshape(num_local, ABLK, slab_piece)
    full_rows = lax.all_gather(local_amp, "beta", axis=2, tiled=True)
    gathered, sources = assemble(full_rows, pair_src, num_local)
    pair_ids = jnp.arange(NP, dtype=jnp.int32)
    pair_hot = (beta_pair[None, :, :] == pair_ids[:, None, None]).astype(jnp.float32)
    looked_up = jnp.einsum("ki,ibj->kbj", integrals, pair_hot, precision=lax.Precision.HIGHEST)
    coupled = (looked_up * beta_coef[None]).astype(jnp.bfloat16)
    link_ids = jnp.arange(LINKS, dtype=jnp.int32)
    string_ids = jnp.arange(ABLK, dtype=jnp.int32)

    def per_target(target, sigma_acc):
        chosen = lax.dynamic_index_in_dim(sources, target, 0, keepdims=False)
        columns = lax.dynamic_index_in_dim(link_col, target, 0, keepdims=False)
        occupied = lax.dynamic_index_in_dim(link_count, target, 0, keepdims=False)
        signs = lax.dynamic_index_in_dim(link_coef, target, 0, keepdims=False)
        targets_row = lax.dynamic_index_in_dim(link_row, target, 0, keepdims=False)

        def per_pair(total, pair_index):
            block = jnp.take(gathered, chosen[pair_index], axis=0)
            column_row = columns[pair_index]
            orbital_pair = column_row // ABLK
            source_row = column_row % ABLK
            amp_rows = jnp.take(block, source_row, axis=0)
            coupled_rows = jnp.take(coupled, orbital_pair, axis=0)
            picked = jnp.einsum(
                "lbj,lj->lb", coupled_rows, amp_rows, preferred_element_type=jnp.float32
            )
            weights = jnp.where(
                link_ids < occupied[pair_index], signs[pair_index], jnp.float32(0.0)
            )
            hot_rows = (targets_row[pair_index][:, None] == string_ids[None, :]).astype(jnp.float32)
            added = jnp.dot(
                hot_rows.T,
                picked * weights[:, None],
                precision=lax.Precision.HIGHEST,
                preferred_element_type=jnp.float32,
            )
            return (total + added, None)

        start = jnp.zeros((ABLK, slab_piece), jnp.float32)
        result, unused = lax.scan(per_pair, start, jnp.arange(chosen.shape[0], dtype=jnp.int32))
        return lax.dynamic_update_index_in_dim(sigma_acc, result, target, 0)

    sigma_acc = jnp.zeros((num_local, ABLK, slab_piece), jnp.float32)
    sigma_acc = lax.fori_loop(0, num_local, per_target, sigma_acc)
    return sigma_acc.reshape(num_local * ABLK, slab_piece)


def body(amplitudes, integrals, beta_pair, beta_coef, pair_src, link_row, link_col, link_coef, link_count):
    anym = pl.BlockSpec(memory_space=pl.ANY)
    smem = pl.BlockSpec(memory_space=pltpu.SMEM)
    vmem = pl.BlockSpec(memory_space=pltpu.VMEM)
    rows = pltpu.VMEM((BLK * PAIRS, LINKS), f32)
    dma = pltpu.SemaphoreType.DMA
    sigma, most = pl.pallas_call(
        kernel,
        out_shape=(
            jax.ShapeDtypeStruct((SLAB, BLK * ABLK), f32),
            jax.ShapeDtypeStruct((1,), f32),
        ),
        in_specs=[anym] * 9,
        out_specs=(vmem, smem),
        scratch_shapes=[
            pltpu.SMEM((PAIRS, ALPHA * BLK), i32),
            pltpu.SMEM((BLK, PAIRS), i32),
            pltpu.VMEM((SLAB, BLK * ABLK), bf16),
            pltpu.VMEM((BLK, SLAB, ABLK), bf16),
            pltpu.VMEM((ALPHA, FETCH_CAP, SLAB, ABLK), bf16),
            pltpu.VMEM((NP, NP), f32),
            pltpu.VMEM((SLAB, NB), i32),
            pltpu.VMEM((SLAB, NB), f32),
            pltpu.VMEM((BLK, PAIRS, LINKS), i32),
            pltpu.VMEM((BLK, PAIRS, LINKS), i32),
            pltpu.VMEM((BLK, PAIRS, LINKS), f32),
            pltpu.VMEM((ALPHA * FETCH_CAP, SLAB, ABLK), bf16),
            pltpu.VMEM((2, SLAB, HALF), f32),
            pltpu.VMEM((NB, HALF), f32),
            pltpu.VMEM((4, BLK, SLAB, PAIRS * ABLK), bf16),
            pltpu.VMEM((NB * KROWS + KROWS, HALF), f32),
            rows, rows, rows, rows, rows, rows,
            pltpu.VMEM((BLK, 128, 128), f32),
            pltpu.VMEM((BLK, 32, 128), f32),
            pltpu.VMEM((GROUPS * 4, BLK * CAP, HALF), bf16),
            pltpu.VMEM((BLK, GROUPS * 4 * CAP, NB), bf16),
            pltpu.VMEM((CHUNKS, 8, SLAB, SPAN * ABLK), f32),
            pltpu.VMEM((CHUNKS, 16, SLAB, SPAN * ABLK), bf16),
            pltpu.VMEM((16, 8, 128), f32),
            dma((9,)), dma((15,)), dma((15,)), dma((7,)), dma((7,)), dma((2,)), dma((2,)),
            dma((2, 2)), dma((2, 2)), dma((CHUNKS, 7)), dma((CHUNKS, 7)), dma((3,)), dma((3,)), dma((6,)), dma((6,)),
        ],
        compiler_params=pltpu.CompilerParams(
            vmem_limit_bytes=60 << 20, collective_id=0, has_side_effects=True
        ),
        name="sigma_links",
    )(amplitudes.T, integrals, beta_pair, beta_coef, pair_src.T, link_col, link_row, link_coef, link_count)
    out = lax.cond(
        most[0] >= CAP,
        lambda: by_links(amplitudes, integrals, beta_pair, beta_coef, pair_src, link_row, link_col, link_coef,
                         link_count).T,
        lambda: sigma,
    )
    return out.T


def solution(mesh):
    in_specs = (P("alpha", "beta"), P(), P("beta", None), P("beta", None), P(),
                P("alpha", None, None), P("alpha", None, None), P("alpha", None, None), P("alpha", None))
    return jax.shard_map(body, mesh=mesh, in_specs=in_specs, out_specs=P("alpha", "beta"), check_vma=False)
```
